32 devices in a mesh: wide: 8 (over z, y), rep: 4 (over x, core).
Axes of the slice: x: 2, y: 2, z: 4, core: 2. Of those that a mesh axis runs over, the one named last changes fastest.
Arguments:
- node_feats: bfloat16 [8192, 512], P('wide'), may hold values from -6 to 6
- w_self: bfloat16 [512, 512], replicated, may hold values from -0.25 to 0.25
- w_neigh: bfloat16 [512, 512], replicated, may hold values from -0.25 to 0.25
- send_rows: int32 [8, 8, 32], P('wide', None, 'rep'), may hold values from 0 to 1023
- tile_dst: int32 [8, 4, 128], P('wide', 'rep'), may hold values from 0 to 15
- tile_src: int32 [8, 4, 128], P('wide', 'rep'), may hold values from 0 to 16
- tile_bits: int32 [8, 4, 32768], P('wide', 'rep'), may hold values from 0 to 65280
- norm_count: int32 [8192], P('wide'), may hold values from 512 to 2048
- grad_out: bfloat16 [8192, 512], P(('wide', 'rep')), may hold values from -6 to 6
Outputs:
- out_feats: bfloat16 [8192, 512], P(('wide', 'rep'))
- grad_feats: bfloat16 [8192, 512], P(('wide', 'rep'))
- grad_self: bfloat16 [512, 512], replicated
- grad_neigh: bfloat16 [512, 512], replicated
The draws below stay inside these ranges and needn't reach their ends.
All inputs are finite; a program needn't handle non-finite values.
Results may differ from the reference program's by a relative error of at most 0.014.
Values may be sent and summed in bfloat16 or wider, within the bound.
A program may use at most 64 MiB of HBM per device.

```python
import jax
import jax.numpy as jnp
from jax import lax

F = 512
BLOCK = 64
NODE_DEV = 1024
SLOT_DEV = 8
TILE_DEV = 128
NODES = 8192
SLOTS = 32
SRC_BLK = 17
WORDS = 32768
N_WIDE = 8
N_REP = 4


def place_ends(entries, rng, least, high):
    dims = entries.shape
    spot = [jax.random.randint(jax.random.fold_in(rng, axis), (), 0, dims[axis]) for axis in range(len(dims))]
    entries = entries.at[tuple(spot)].set(least)
    longest = dims.index(max(dims))
    spot[longest] = (spot[longest] + 1) % dims[longest]
    return entries.at[tuple(spot)].set(high)


def shard_levels(own_key, shape, shards, smallest, largest):
    def one(dim, blocks):
        steps = jax.random.uniform(jax.random.fold_in(jax.random.fold_in(own_key, 6), dim), (blocks,), jnp.float32, smallest / len(shards), largest / len(shards))
        return jnp.repeat(jnp.exp(steps), shape[dim] // blocks).reshape((-1,) + (1,) * (len(shape) - dim - 1))

    gain = one(*shards[0])
    for cut in shards[1:]:
        gain = gain * one(*cut)
    return gain


def centred(own_key, dims, scale, limit, split=(), held_as=jnp.bfloat16):
    result = jax.random.normal(own_key, dims, jnp.float32) * scale
    if len(split) > 0:
        result = shard_levels(own_key, dims, split, -0.22, 0.18) * result
    return jnp.clip(result, min=-limit, max=limit).astype(held_as)


def setup_inputs(seed: int = 0) -> dict:
    seeds = jax.random.split(jax.random.key(seed), 10)
    return {
        "node_feats": centred(seeds[0], (NODES, F), 1.0, 6.0, ((0, 8),)),
        "w_self": centred(seeds[1], (F, F), F ** -0.5, 0.25),
        "w_neigh": centred(seeds[2], (F, F), F ** -0.5, 0.25),
        "send_rows": place_ends(jax.random.randint(seeds[3], (N_WIDE, N_WIDE, SLOTS), 0, NODE_DEV), jax.random.fold_in(seeds[3], 1), 0, NODE_DEV - 1).astype(jnp.int32),
        "tile_dst": place_ends(jax.random.randint(seeds[4], (N_WIDE, N_REP, TILE_DEV), 0, NODE_DEV // BLOCK), jax.random.fold_in(seeds[4], 1), 0, (NODE_DEV // BLOCK) - 1).astype(jnp.int32),
        "tile_src": place_ends(jax.random.randint(seeds[5], (N_WIDE, N_REP, TILE_DEV), 0, SRC_BLK), jax.random.fold_in(seeds[5], 1), 0, SRC_BLK - 1).astype(jnp.int32),
        "tile_bits": place_ends(jax.random.randint(seeds[6], (N_WIDE, N_REP, WORDS), 0, 65281), jax.random.fold_in(seeds[6], 1), 0, 65280).astype(jnp.int32),
        "norm_count": place_ends(jax.random.randint(seeds[7], (NODES,), max(1, TILE_DEV * N_REP * BLOCK * BLOCK // (4 * NODE_DEV)), TILE_DEV * N_REP * BLOCK * BLOCK // NODE_DEV + 1), jax.random.fold_in(seeds[7], 1), max(1, TILE_DEV * N_REP * BLOCK * BLOCK // (4 * NODE_DEV)), (TILE_DEV * N_REP * BLOCK * BLOCK // NODE_DEV + 1) - 1).astype(jnp.int32),
        "grad_out": centred(seeds[8], (NODES, F), 1.0, 6.0, ((0, 32),)),
    }


def unpack_bits(packed, tile_count):
    shaped = packed.reshape(tile_count, BLOCK, BLOCK // 16)
    shift_list = jnp.arange(16, dtype=jnp.int32)
    bit_grid = jnp.bitwise_and(jnp.right_shift(shaped[..., None], shift_list), 1)
    return bit_grid.reshape(tile_count, BLOCK, BLOCK).astype(jnp.float32)

def build_table(per_device, send_rows, wide_index, rep_index):
    owners = jnp.arange(N_WIDE, dtype=jnp.int32)[:, None]
    column = jnp.take(send_rows, wide_index, axis=1)
    slot_rows = column[:, rep_index * SLOT_DEV:(rep_index + 1) * SLOT_DEV]
    halo_rows = per_device[owners, slot_rows]
    src_table = jnp.concatenate([per_device[wide_index], halo_rows.reshape(N_WIDE * SLOT_DEV, F)], axis=0)
    targets = (owners * NODE_DEV + slot_rows).reshape(-1)
    return (src_table, targets)

def reference(node_feats, w_self, w_neigh, send_rows, tile_dst, tile_src, tile_bits, norm_count, grad_out):
    per_device = node_feats.reshape(N_WIDE, NODE_DEV, F)
    dst_count = NODE_DEV // BLOCK

    def aggregate(wide_index):
        running = jnp.zeros((dst_count, BLOCK, F), jnp.float32)
        for rep_index in range(N_REP):
            src_table, _ = build_table(per_device, send_rows, wide_index, rep_index)
            blocks = src_table.reshape(SRC_BLK, BLOCK, F).astype(jnp.float32)
            tile_masks = unpack_bits(tile_bits[wide_index, rep_index], TILE_DEV)
            picked = blocks[tile_src[wide_index, rep_index]]
            products = jnp.einsum('tij,tjf->tif', tile_masks, picked, precision=lax.Precision.HIGHEST)
            running = running.at[tile_dst[wide_index, rep_index]].add(products)
        return running.reshape(NODE_DEV, F)
    neigh_sums = lax.map(aggregate, jnp.arange(N_WIDE, dtype=jnp.int32)).reshape(NODES, F)
    row_scale = lax.rsqrt(norm_count.astype(jnp.float32))
    agg_rows = (neigh_sums * row_scale[:, None]).astype(jnp.bfloat16)
    pre_act = jnp.dot(node_feats, w_self, preferred_element_type=jnp.float32) + jnp.dot(agg_rows, w_neigh, preferred_element_type=jnp.float32)
    sigmoid = jax.nn.sigmoid(pre_act)
    out_feats = (pre_act * sigmoid).astype(jnp.bfloat16)
    grad_pre = (grad_out.astype(jnp.float32) * sigmoid * (1.0 + pre_act * (1.0 - sigmoid))).astype(jnp.bfloat16)
    grad_self = jnp.dot(node_feats.T, grad_pre, preferred_element_type=jnp.float32).astype(jnp.bfloat16)
    grad_neigh = jnp.dot(agg_rows.T, grad_pre, preferred_element_type=jnp.float32).astype(jnp.bfloat16)
    grad_agg = (jnp.dot(grad_pre, w_neigh.T, preferred_element_type=jnp.float32) * row_scale[:, None]).astype(jnp.bfloat16)
    agg_blocks = grad_agg.reshape(N_WIDE, dst_count, BLOCK, F)

    def spread(grad_rows, wide_index):
        for rep_index in range(N_REP):
            _, targets = build_table(per_device, send_rows, wide_index, rep_index)
            tile_masks = unpack_bits(tile_bits[wide_index, rep_index], TILE_DEV)
            picked = agg_blocks[wide_index][tile_dst[wide_index, rep_index]].astype(jnp.float32)
            products = jnp.einsum('tij,tif->tjf', tile_masks, picked, precision=lax.Precision.HIGHEST)
            table_grad = jnp.zeros((SRC_BLK, BLOCK, F), jnp.float32).at[tile_src[wide_index, rep_index]].add(products)
            table_grad = table_grad.reshape(SRC_BLK * BLOCK, F)
            own_rows = lax.dynamic_slice_in_dim(grad_rows, wide_index * NODE_DEV, NODE_DEV, 0)
            grad_rows = lax.dynamic_update_slice_in_dim(grad_rows, own_rows + table_grad[:NODE_DEV], wide_index * NODE_DEV, 0)
            rounded = lax.optimization_barrier(table_grad[NODE_DEV:].astype(jnp.bfloat16))
            grad_rows = grad_rows.at[targets].add(rounded.astype(jnp.float32))
        return (grad_rows, None)
    grad_rows, _ = lax.scan(spread, jnp.zeros((NODES, F), jnp.float32), jnp.arange(N_WIDE, dtype=jnp.int32))
    grad_feats = (grad_rows + jnp.dot(grad_pre, w_self.T, preferred_element_type=jnp.float32)).astype(jnp.bfloat16)
    return (out_feats, grad_feats, grad_self, grad_neigh)
```

```python
import functools

import jax
import jax.numpy as jnp
from jax import lax
from jax.experimental import pallas as pl
from jax.experimental.pallas import tpu as pltpu
from jax.sharding import PartitionSpec as P

BLOCK = 64
GROUP = 32
LANES = 128
MESH = pl.DeviceIdType.MESH
VMEM_BYTES = 56 * 1024 * 1024


def partners(replicas):
    mine = lax.axis_index("rep")
    core = mine + 1 - 2 * lax.rem(mine, 2)
    across = lax.rem(mine + 2, replicas)
    diagonal = lax.rem(core + 2, replicas)
    return mine, core, across, diagonal


def enter(peer_count, mine_wide, mine, core, across):
    barrier = pltpu.get_barrier_semaphore()
    for step in range(1, peer_count):
        peer = lax.rem(mine_wide + step, peer_count)
        pl.semaphore_signal(barrier, inc=1, device_id=(peer, mine), device_id_type=MESH)
    for other in (core, across):
        pl.semaphore_signal(barrier, inc=1, device_id=(mine_wide, other), device_id_type=MESH)
    pl.semaphore_wait(barrier, peer_count + 1)


def times_transposed(left, right):
    return lax.dot_general(
        left, right, (((1,), (1,)), ((), ())), preferred_element_type=jnp.float32
    )


def transposed_times(left, right):
    return lax.dot_general(
        left, right, (((0,), (0,)), ((), ())), preferred_element_type=jnp.float32
    )


def spread_inputs(
    peer_count,
    slots,
    bits,
    meta,
    grad_out,
    index_col,
    feats,
    all_bits,
    all_meta,
    all_grad,
    all_halo,
    outgoing,
    local_sem,
    send_sem,
    recv_sem,
    halo_send,
    halo_recv,
):
    mine_wide = lax.axis_index("wide")
    mine, core, across, diagonal = partners(4)
    enter(peer_count, mine_wide, mine, core, across)

    def push(src, dst, which, wide_to, rep_to):
        return pltpu.make_async_remote_copy(
            src_ref=src,
            dst_ref=dst,
            send_sem=send_sem.at[which],
            recv_sem=recv_sem.at[which],
            device_id=(wide_to, rep_to),
            device_id_type=MESH,
        )

    pairs = ((bits, all_bits), (meta, all_meta), (grad_out, all_grad))
    to_across = [
        push(src, dst.at[mine], n, mine_wide, across) for n, (src, dst) in enumerate(pairs)
    ]
    to_core = [
        push(src, dst.at[mine], 4 + n, mine_wide, core) for n, (src, dst) in enumerate(pairs)
    ]
    own = [
        pltpu.make_async_copy(src, dst.at[mine], local_sem.at[n])
        for n, (src, dst) in enumerate(pairs)
    ]
    for copy in to_across + to_core + own:
        copy.start()
    node_rows = feats.shape[0]
    half = feats.shape[1] // 2
    for first in range(0, peer_count * slots, 64):
        picks = index_col[first : first + 64, :]
        chosen = picks == lax.broadcasted_iota(jnp.int32, (64, node_rows), 1)
        rows = jnp.dot(
            chosen.astype(jnp.bfloat16), feats[...], preferred_element_type=jnp.float32
        )
        for n in range(64 // slots):
            part = rows[n * slots : (n + 1) * slots]
            outgoing[first // slots + n] = jnp.concatenate(
                [part[:, :half], part[:, half:]], axis=0
            ).astype(jnp.bfloat16)
    exchange = []
    for step in range(1, peer_count):
        peer = lax.rem(mine_wide + step, peer_count)
        copy = pltpu.make_async_remote_copy(
            src_ref=outgoing.at[peer],
            dst_ref=all_halo.at[mine, mine_wide],
            send_sem=halo_send.at[step],
            recv_sem=halo_recv.at[step],
            device_id=(peer, mine),
            device_id_type=MESH,
        )
        copy.start()
        exchange.append(copy)
    kept = pltpu.make_async_copy(
        outgoing.at[mine_wide], all_halo.at[mine, mine_wide], local_sem.at[3]
    )
    kept.start()
    kept.wait()
    for copy in exchange:
        copy.wait_recv()
    halo_across = push(all_halo.at[mine], all_halo.at[mine], 3, mine_wide, across)
    halo_core = push(all_halo.at[mine], all_halo.at[mine], 7, mine_wide, core)
    halo_across.start()
    halo_core.start()
    onward = []
    for n, (came, dst) in enumerate(
        zip(to_across + [halo_across], (all_bits, all_meta, all_grad, all_halo))
    ):
        came.wait_recv()
        copy = push(dst.at[across], dst.at[across], 8 + n, mine_wide, core)
        copy.start()
        onward.append(copy)
    for copy in to_core + [halo_core] + onward:
        copy.wait_recv()
    for copy in to_across + to_core + [halo_across, halo_core] + onward + exchange:
        copy.wait_send()
    for copy in own:
        copy.wait()


def layer(
    peer_count,
    slots,
    meta,
    bits,
    grad_out,
    halo,
    feats,
    w_self,
    w_neigh,
    norm,
    out_feats,
    own_grad,
    halo_grad,
    weight_grad,
    blocks,
    adjacency,
    table,
    lhs,
    scale,
    agg,
    grad_pre,
    grad_agg,
):
    replicas = bits.shape[0]
    mine = lax.axis_index("rep")
    node_rows, width = feats.shape
    half = width // 2
    dst_count = node_rows // BLOCK
    halo_rows = peer_count * slots
    halo_blocks = halo_rows // BLOCK
    pair_count = (dst_count + replicas * halo_blocks) // 2
    groups = bits.shape[1] // BLOCK
    quarter = node_rows // replicas

    blocks[...] = jnp.zeros_like(blocks)
    for r in range(replicas):
        words = bits[r]
        rows = pl.ds(r * words.shape[0], words.shape[0])
        lhs[rows, :LANES] = (words & 255).astype(jnp.float32).astype(jnp.bfloat16)
        lhs[rows, LANES:] = (words >> 8).astype(jnp.float32).astype(jnp.bfloat16)

    row = lax.broadcasted_iota(jnp.int32, (2 * LANES, 2 * LANES), 0)
    col = lax.broadcasted_iota(jnp.int32, (2 * LANES, 2 * LANES), 1)
    bit = col & (BLOCK - 1)
    match = (((row >> 5) & 3) == (bit >> 4)) & ((row >> 7) == ((bit >> 3) & 1))
    factor = (1 << (7 - (bit & 7))).astype(jnp.float32) * (1.0 / 128.0)
    pattern = jnp.where(match, factor, 0.0)
    behind = (row & (GROUP - 1)) - (col >> 7)
    lane_half = lax.broadcasted_iota(jnp.int32, (BLOCK, LANES), 1) >> 6

    def two_tiles(n, carry):
        chosen = jnp.where(behind == 2 * n, pattern, 0.0).astype(jnp.bfloat16)
        raised = jnp.dot(lhs[...], chosen, preferred_element_type=jnp.float32).astype(jnp.int32)
        for r in range(replicas):
            for g in range(groups):
                for t in range(2):
                    place = g * GROUP + 2 * n + t
                    dst = meta[r, 0, place]
                    src = meta[r, 1, place]
                    column = jnp.where(src < dst_count, src, src + r * halo_blocks)
                    where = dst * pair_count + (column >> 1)
                    keep = jnp.where(lane_half == (column & 1), 1, 0)
                    first = (r * groups + g) * BLOCK
                    part = raised[first : first + BLOCK, t * LANES : (t + 1) * LANES]
                    blocks[where] += (part & keep).astype(jnp.float32)
        return carry

    lax.fori_loop(0, GROUP // 2, two_tiles, 0)

    def place_row(b, carry):
        rows = pl.ds(pl.multiple_of(b * BLOCK, BLOCK), BLOCK)
        for p in range(pair_count):
            adjacency[rows, p * LANES : (p + 1) * LANES] = blocks[b * pair_count + p].astype(
                jnp.bfloat16
            )
        return carry

    lax.fori_loop(0, dst_count, place_row, 0)

    table[:node_rows, :] = feats[...]
    for r in range(replicas):
        for first in range(0, peer_count, 8):
            part = halo[r, first : first + 8].astype(jnp.float32)
            joined = jnp.concatenate([part[:, :slots, :], part[:, slots:, :]], axis=2)
            start = node_rows + r * halo_rows + first * slots
            table[start : start + 8 * slots, :] = joined.reshape(8 * slots, width).astype(
                jnp.bfloat16
            )

    eye = lax.broadcasted_iota(jnp.int32, (LANES, LANES), 0) == lax.broadcasted_iota(
        jnp.int32, (LANES, LANES), 1
    )
    for n in range(node_rows // LANES):
        counts = norm[n : n + 1, :].astype(jnp.float32)
        column = jnp.sum(jnp.where(eye, counts, 0.0), axis=1, keepdims=True)
        scale[n * LANES : (n + 1) * LANES, :] = lax.rsqrt(column)

    def forward(q, carry):
        rows = pl.ds(pl.multiple_of(q * quarter, quarter), quarter)
        sums = jnp.dot(adjacency[rows, :], table[...], preferred_element_type=jnp.float32)
        part_scale = scale[rows, :]
        part_agg = (sums * part_scale).astype(jnp.bfloat16)
        agg[rows, :] = part_agg
        pre = jnp.dot(feats[rows, :], w_self[...], preferred_element_type=jnp.float32) + jnp.dot(
            part_agg, w_neigh[...], preferred_element_type=jnp.float32
        )
        sig = jax.nn.sigmoid(pre)

        @pl.when(q == mine)
        def _():
            out_feats[...] = (pre * sig).astype(jnp.bfloat16)

        back = (grad_out[q].astype(jnp.float32) * sig * (1.0 + pre * (1.0 - sig))).astype(
            jnp.bfloat16
        )
        grad_pre[rows, :] = back
        grad_agg[rows, :] = (times_transposed(back, w_neigh[...]) * part_scale).astype(
            jnp.bfloat16
        )
        return carry

    lax.fori_loop(0, replicas, forward, 0)

    share = width // replicas
    columns = pl.ds(pl.multiple_of(mine * share, share), share)
    weight_grad[:share, :] = transposed_times(feats[:, columns], grad_pre[...]).astype(
        jnp.bfloat16
    )
    weight_grad[share:, :] = transposed_times(agg[:, columns], grad_pre[...]).astype(jnp.bfloat16)

    for r in range(replicas):
        start = node_rows + r * halo_rows
        step = min(halo_rows, 512)
        for first in range(0, halo_rows, step):
            part = transposed_times(
                adjacency[:, start + first : start + first + step], grad_agg[...]
            )
            for n in range(step // slots):
                halo_grad[first // slots + n, r * slots : (r + 1) * slots, :] = part[
                    n * slots : (n + 1) * slots
                ].astype(jnp.bfloat16)

    own_rows = pl.ds(pl.multiple_of(mine * quarter, quarter), quarter)
    own_grad[...] = transposed_times(adjacency[:, own_rows], grad_agg[...]) + times_transposed(
        grad_pre[own_rows, :], w_self[...]
    )


def finish(
    peer_count,
    reduce_here,
    halo_grad,
    weight_grad,
    own_grad,
    targets,
    grad_feats,
    weights,
    came_halo,
    came_weight,
    summed,
    local_sem,
    halo_send,
    halo_recv,
    part_send,
    part_recv,
    full_send,
    full_recv,
    rep_send,
    rep_recv,
):
    mine_wide = lax.axis_index("wide")
    mine, core, across, diagonal = partners(4)
    enter(peer_count, mine_wide, mine, core, across)
    quarter = own_grad.shape[0]
    rows = weight_grad.shape[0] // peer_count
    per_half = peer_count // 2
    share = weight_grad.shape[0] // 2

    def push(src, dst, send, recv, wide_to, rep_to):
        copy = pltpu.make_async_remote_copy(
            src_ref=src,
            dst_ref=dst,
            send_sem=send,
            recv_sem=recv,
            device_id=(wide_to, rep_to),
            device_id_type=MESH,
        )
        copy.start()
        return copy

    def place(owner_wide, owner_rep):
        start = owner_rep * share + lax.rem(owner_wide, per_half) * rows
        return weights.at[owner_wide // per_half, pl.ds(pl.multiple_of(start, rows), rows)]

    part_copies, halo_copies, full_copies = [], [], []
    if reduce_here:
        for step in range(1, peer_count):
            peer = lax.rem(mine_wide + step, peer_count)
            piece = weight_grad.at[pl.ds(pl.multiple_of(peer * rows, rows), rows)]
            part_copies.append(
                push(
                    piece, came_weight.at[step], part_send.at[step], part_recv.at[step], peer, mine
                )
            )
    for step in range(1, peer_count):
        peer = lax.rem(mine_wide + step, peer_count)
        halo_copies.append(
            push(
                halo_grad.at[peer],
                came_halo.at[mine_wide],
                halo_send.at[step],
                halo_recv.at[step],
                peer,
                mine,
            )
        )
    kept = pltpu.make_async_copy(halo_grad.at[mine_wide], came_halo.at[mine_wide], local_sem.at[0])
    kept.start()
    if reduce_here:
        total = weight_grad[pl.ds(pl.multiple_of(mine_wide * rows, rows), rows), :].astype(
            jnp.float32
        )
        for step in range(1, peer_count):
            part_copies[step - 1].wait_recv()
            total = total + came_weight[step].astype(jnp.float32)
        summed[...] = total.astype(jnp.bfloat16)
        spot = place(mine_wide, mine)
        for step in range(1, peer_count):
            peer = lax.rem(mine_wide + step, peer_count)
            full_copies.append(
                push(summed, spot, full_send.at[step], full_recv.at[step], peer, mine)
            )
        across_copies = [
            push(summed, spot, rep_send.at[0, 0], rep_recv.at[0, 0], mine_wide, across)
        ]
        core_copies = [push(summed, spot, rep_send.at[1, 0], rep_recv.at[1, 0], mine_wide, core)]
        own_slice = pltpu.make_async_copy(summed, spot, local_sem.at[1])
        own_slice.start()

    kept.wait()
    for copy in halo_copies:
        copy.wait_recv()
    count = targets.shape[1]
    total = own_grad[...]
    block = min(count, 512)
    for first in range(0, count, block):
        chosen = targets[:, first : first + block] - mine * quarter == lax.broadcasted_iota(
            jnp.int32, (quarter, block), 0
        )
        per = block // came_halo.shape[1]
        got = came_halo[first // came_halo.shape[1] : first // came_halo.shape[1] + per].reshape(
            block, came_halo.shape[2]
        )
        total = total + jnp.dot(
            chosen.astype(jnp.bfloat16), got, preferred_element_type=jnp.float32
        )
    grad_feats[...] = total.astype(jnp.bfloat16)

    if reduce_here:
        for step in range(1, peer_count):
            full_copies[step - 1].wait_recv()
            owner = lax.rem(mine_wide + peer_count - step, peer_count)
            spot = place(owner, mine)
            across_copies.append(
                push(spot, spot, rep_send.at[0, step], rep_recv.at[0, step], mine_wide, across)
            )
            core_copies.append(
                push(spot, spot, rep_send.at[1, step], rep_recv.at[1, step], mine_wide, core)
            )
        onward = []
        for step in range(peer_count):
            across_copies[step].wait_recv()
            owner = lax.rem(mine_wide + peer_count - step, peer_count)
            spot = place(owner, across)
            onward.append(
                push(spot, spot, rep_send.at[2, step], rep_recv.at[2, step], mine_wide, core)
            )
        for copy in core_copies + onward:
            copy.wait_recv()
        for copy in part_copies + full_copies + across_copies + core_copies + onward:
            copy.wait_send()
        own_slice.wait()
    for copy in halo_copies:
        copy.wait_send()


def on_device(
    node_feats, w_self, w_neigh, send_rows, tile_dst, tile_src, tile_bits, norm_count, grad_out
):
    node_rows, width = node_feats.shape
    peer_count = lax.axis_size("wide")
    replicas = lax.axis_size("rep")
    slots = send_rows.shape[2]
    tile_total = tile_dst.shape[2]
    quarter = node_rows // replicas
    halo_rows = peer_count * slots
    halo_blocks = halo_rows // BLOCK
    words = BLOCK // 16
    groups = tile_total // GROUP

    bits = (
        tile_bits.reshape(groups, GROUP, BLOCK, words)
        .transpose(0, 2, 3, 1)
        .reshape(groups * BLOCK, words * GROUP)
    )
    send_flat = send_rows.reshape(-1)
    meta = jnp.concatenate(
        [tile_dst.reshape(1, -1), tile_src.reshape(1, -1)]
        + [jnp.zeros((6, tile_total), jnp.int32)],
        axis=0,
    )
    send_tiles = jnp.pad(send_flat, (0, -send_flat.shape[0] % (8 * LANES))).reshape(-1, LANES)
    meta = jnp.concatenate([meta, send_tiles], axis=0)
    any_spec = pl.BlockSpec(memory_space=pl.ANY)
    vmem_spec = pl.BlockSpec(memory_space=pltpu.VMEM)
    smem_spec = pl.BlockSpec(memory_space=pltpu.SMEM)

    def shaped(dims, held):
        return jax.ShapeDtypeStruct(dims, held)

    with jax.named_scope("spread_inputs"):
        all_bits, all_meta, all_grad, all_halo = pl.pallas_call(
            functools.partial(spread_inputs, peer_count, slots),
            out_shape=(
                shaped((replicas,) + bits.shape, jnp.int32),
                shaped((replicas,) + meta.shape, jnp.int32),
                shaped((replicas,) + grad_out.shape, jnp.bfloat16),
                shaped((replicas, peer_count, 2 * slots, width // 2), jnp.bfloat16),
            ),
            in_specs=[any_spec] * 3 + [vmem_spec] * 2,
            out_specs=(any_spec,) * 4,
            scratch_shapes=[
                pltpu.VMEM((peer_count, 2 * slots, width // 2), jnp.bfloat16),
                pltpu.SemaphoreType.DMA((4,)),
                pltpu.SemaphoreType.DMA((12,)),
                pltpu.SemaphoreType.DMA((12,)),
                pltpu.SemaphoreType.DMA((peer_count,)),
                pltpu.SemaphoreType.DMA((peer_count,)),
            ],
            compiler_params=pltpu.CompilerParams(
                collective_id=0, has_side_effects=True, vmem_limit_bytes=VMEM_BYTES
            ),
        )(bits, meta, grad_out, send_flat.reshape(-1, 1), node_feats)

    columns = node_rows + replicas * halo_rows
    pair_count = columns // LANES
    dst_count = node_rows // BLOCK
    with jax.named_scope("layer"):
        out_feats, own_grad, halo_grad, weight_grad = pl.pallas_call(
            functools.partial(layer, peer_count, slots),
            out_shape=(
                shaped((quarter, width), jnp.bfloat16),
                shaped((quarter, width), jnp.float32),
                shaped((peer_count, replicas * slots, width), jnp.bfloat16),
                shaped((2 * width // replicas, width), jnp.bfloat16),
            ),
            in_specs=[smem_spec] + [vmem_spec] * 7,
            out_specs=(vmem_spec,) * 4,
            scratch_shapes=[
                pltpu.VMEM((dst_count * pair_count, BLOCK, LANES), jnp.float32),
                pltpu.VMEM((node_rows, columns), jnp.bfloat16),
                pltpu.VMEM((columns, width), jnp.bfloat16),
                pltpu.VMEM((replicas * groups * BLOCK, 2 * LANES), jnp.bfloat16),
                pltpu.VMEM((node_rows, 1), jnp.float32),
                pltpu.VMEM((node_rows, width), jnp.bfloat16),
                pltpu.VMEM((node_rows, width), jnp.bfloat16),
                pltpu.VMEM((node_rows, width), jnp.bfloat16),
            ],
            compiler_params=pltpu.CompilerParams(vmem_limit_bytes=VMEM_BYTES),
        )(
            all_meta,
            all_bits,
            all_grad,
            all_halo,
            node_feats,
            w_self,
            w_neigh,
            norm_count.reshape(-1, LANES),
        )

    targets = (
        all_meta[:, 8:, :]
        .reshape(replicas, -1)[:, :halo_rows]
        .reshape(replicas, peer_count, slots)
        .transpose(1, 0, 2)
        .reshape(1, -1)
    )
    rows = weight_grad.shape[0] // peer_count
    reduce_here = rows % 16 == 0
    piece = (rows if reduce_here else 16, width)
    with jax.named_scope("finish"):
        grad_feats, weights = pl.pallas_call(
            functools.partial(finish, peer_count, reduce_here),
            out_shape=(
                shaped((quarter, width), jnp.bfloat16),
                shaped((2, width, width), jnp.bfloat16),
            ),
            in_specs=[vmem_spec] * 4,
            out_specs=(vmem_spec, any_spec),
            scratch_shapes=[
                pltpu.VMEM((peer_count, replicas * slots, width), jnp.bfloat16),
                pltpu.VMEM((peer_count,) + piece, jnp.bfloat16),
                pltpu.VMEM(piece, jnp.bfloat16),
                pltpu.SemaphoreType.DMA((2,)),
            ]
            + [pltpu.SemaphoreType.DMA((peer_count,))] * 6
            + [pltpu.SemaphoreType.DMA((3, peer_count))] * 2,
            compiler_params=pltpu.CompilerParams(
                collective_id=1, has_side_effects=True, vmem_limit_bytes=VMEM_BYTES
            ),
        )(halo_grad, weight_grad, own_grad, targets)
    if reduce_here:
        return out_feats, grad_feats, weights[0], weights[1]
    total = lax.psum(weight_grad.astype(jnp.float32), "wide").astype(jnp.bfloat16)
    whole = lax.all_gather(total, "rep", axis=0, tiled=False)
    share = width // replicas
    return (
        out_feats,
        grad_feats,
        whole[:, :share].reshape(width, width),
        whole[:, share:].reshape(width, width),
    )


def solution(mesh):
    in_specs = (
        P("wide", None),
        P(),
        P(),
        P("wide", None, "rep"),
        P("wide", "rep", None),
        P("wide", "rep", None),
        P("wide", "rep", None),
        P("wide"),
        P(("wide", "rep"), None),
    )
    out_specs = (P(("wide", "rep"), None), P(("wide", "rep"), None), P(), P())
    return jax.shard_map(
        on_device, mesh=mesh, in_specs=in_specs, out_specs=out_specs, check_vma=False
    )
```

```python
import functools

import jax
import jax.numpy as jnp
from jax import lax
from jax.experimental import pallas as pl
from jax.experimental.pallas import tpu as pltpu
from jax.sharding import PartitionSpec as P

BLOCK = 64
GROUP = 32
LANES = 128
MESH = pl.DeviceIdType.MESH
VMEM_BYTES = 56 * 1024 * 1024


def partners(replicas):
    mine = lax.axis_index("rep")
    core = mine + 1 - 2 * lax.rem(mine, 2)
    across = lax.rem(mine + 2, replicas)
    diagonal = lax.rem(core + 2, replicas)
    return mine, core, across, diagonal


def times_transposed(left, right):
    return lax.dot_general(
        left, right, (((1,), (1,)), ((), ())), preferred_element_type=jnp.float32
    )


def transposed_times(left, right):
    return lax.dot_general(
        left, right, (((0,), (0,)), ((), ())), preferred_element_type=jnp.float32
    )


def as_column(picks):
    count, slots = picks.shape
    same = lax.broadcasted_iota(jnp.int32, (count, slots, slots), 1) == lax.broadcasted_iota(
        jnp.int32, (count, slots, slots), 2
    )
    wide = jnp.broadcast_to(picks.astype(jnp.float32)[:, None, :], (count, slots, slots))
    column = jnp.sum(jnp.where(same, wide, 0.0), axis=2, keepdims=True)
    return column.reshape(count * slots, 1).astype(jnp.int32)


def folded(part):
    half = part.shape[1] // 2
    return jnp.concatenate([part[:, :half], part[:, half:]], axis=0).astype(jnp.bfloat16)


def unfolded(parts):
    count, rows, half = parts.shape
    wide = parts.astype(jnp.float32)
    joined = jnp.concatenate([wide[:, : rows // 2, :], wide[:, rows // 2 :, :]], axis=2)
    return joined.reshape(count * rows // 2, 2 * half).astype(jnp.bfloat16)


def sort_words(words, sorted_words):
    rows = lax.broadcasted_iota(jnp.int32, (LANES, LANES), 0)
    lanes = lax.broadcasted_iota(jnp.int32, (LANES, LANES), 1)
    wanted = (rows // GROUP) == lanes % 4
    pick_row = lax.broadcasted_iota(jnp.int32, (GROUP, 2 * LANES), 0)
    pick_lane = lax.broadcasted_iota(jnp.int32, (GROUP, 2 * LANES), 1) % LANES
    pick = jnp.where(pick_row == pick_lane // 4, 1.0, 0.0).astype(jnp.bfloat16)
    for group in range(words.shape[0] // BLOCK):
        for h in range(2):
            part = words[pl.ds(group * BLOCK + h, GROUP, stride=2), :]
            low = (part & 255).astype(jnp.float32)
            high = (part - (part & 255)).astype(jnp.float32)
            both = jnp.concatenate(
                [
                    jnp.where(wanted, jnp.concatenate([half] * 4, axis=0), 0.0)
                    for half in (low, high)
                ],
                axis=1,
            ).astype(jnp.bfloat16)
            start = group * BLOCK + h * GROUP
            sorted_words[start : start + GROUP, :] = times_transposed(pick, both).astype(jnp.int32)


def greet(peer_count, mine_wide, mine, core, across):
    barrier = pltpu.get_barrier_semaphore()
    for step in range(1, peer_count):
        peer = lax.rem(mine_wide + step, peer_count)
        pl.semaphore_signal(barrier, inc=1, device_id=(peer, mine), device_id_type=MESH)
    for other in (core, across):
        pl.semaphore_signal(barrier, inc=1, device_id=(mine_wide, other), device_id_type=MESH)
    return barrier


def push(src, dst, send, recv, wide_to, rep_to):
    copy = pltpu.make_async_remote_copy(
        src_ref=src,
        dst_ref=dst,
        send_sem=send,
        recv_sem=recv,
        device_id=(wide_to, rep_to),
        device_id_type=MESH,
    )
    copy.start()
    return copy


def spread_inputs(
    peer_count,
    slots,
    words,
    tile_dst,
    tile_src,
    send_rows,
    feats,
    all_bits,
    all_meta,
    all_halo,
    bits,
    meta,
    outgoing,
    local_sem,
    send_sem,
    recv_sem,
    halo_send,
    halo_recv,
):
    mine_wide = lax.axis_index("wide")
    mine, core, across, diagonal = partners(4)
    barrier = greet(peer_count, mine_wide, mine, core, across)
    meta[...] = jnp.zeros_like(meta)
    meta[0:1, :] = tile_dst[...]
    meta[1:2, :] = tile_src[...]
    meta[8:, :slots] = send_rows[...]
    node_rows = feats.shape[0]
    for first in range(0, peer_count, 8):
        picks = as_column(send_rows[first : first + 8, :])
        chosen = picks == lax.broadcasted_iota(jnp.int32, (8 * slots, node_rows), 1)
        rows = jnp.dot(
            jnp.where(chosen, 1.0, 0.0).astype(jnp.bfloat16),
            feats[...],
            preferred_element_type=jnp.float32,
        )
        for n in range(8):
            outgoing[first + n] = folded(rows[n * slots : (n + 1) * slots])
    sort_words(words, bits)
    pl.semaphore_wait(barrier, peer_count + 1)

    exchange = []
    for step in range(1, peer_count):
        peer = lax.rem(mine_wide + step, peer_count)
        exchange.append(
            push(
                outgoing.at[peer],
                all_halo.at[mine, mine_wide],
                halo_send.at[step],
                halo_recv.at[step],
                peer,
                mine,
            )
        )
    pairs = ((bits, all_bits), (meta, all_meta))
    to_across = [
        push(src, dst.at[mine], send_sem.at[n], recv_sem.at[n], mine_wide, across)
        for n, (src, dst) in enumerate(pairs)
    ]
    to_core = [
        push(src, dst.at[mine], send_sem.at[3 + n], recv_sem.at[3 + n], mine_wide, core)
        for n, (src, dst) in enumerate(pairs)
    ]
    own = [
        pltpu.make_async_copy(src, dst.at[mine], local_sem.at[n])
        for n, (src, dst) in enumerate(pairs)
    ]
    kept = pltpu.make_async_copy(
        outgoing.at[mine_wide], all_halo.at[mine, mine_wide], local_sem.at[2]
    )
    for copy in own + [kept]:
        copy.start()
    kept.wait()
    for copy in exchange:
        copy.wait_recv()
    block = all_halo.at[mine]
    to_across.append(push(block, block, send_sem.at[2], recv_sem.at[2], mine_wide, across))
    to_core.append(push(block, block, send_sem.at[5], recv_sem.at[5], mine_wide, core))
    onward = []
    for n, dst in enumerate((all_bits, all_meta, all_halo)):
        to_across[n].wait_recv()
        block = dst.at[across]
        onward.append(push(block, block, send_sem.at[6 + n], recv_sem.at[6 + n], mine_wide, core))
    for copy in to_core + onward:
        copy.wait_recv()
    for copy in to_across + to_core + onward + exchange:
        copy.wait_send()
    for copy in own:
        copy.wait()


def build_adjacency(dst_count, halo_blocks, meta, bits, adjacency, blocks, lhs):
    replicas = bits.shape[0]
    pair_count = (dst_count + replicas * halo_blocks) // 2
    groups = bits.shape[1] // BLOCK

    blocks[...] = jnp.zeros_like(blocks)
    for r in range(replicas):
        words = bits[r]
        rows = pl.ds(r * words.shape[0], words.shape[0])
        lhs[rows, :LANES] = (words & 255).astype(jnp.float32).astype(jnp.bfloat16)
        lhs[rows, LANES:] = (words >> 8).astype(jnp.float32).astype(jnp.bfloat16)

    row = lax.broadcasted_iota(jnp.int32, (2 * LANES, 2 * LANES), 0)
    col = lax.broadcasted_iota(jnp.int32, (2 * LANES, 2 * LANES), 1)
    bit = col & (BLOCK - 1)
    match = (((row >> 5) & 3) == (bit >> 4)) & ((row >> 7) == ((bit >> 3) & 1))
    factor = (1 << (7 - (bit & 7))).astype(jnp.float32) * (1.0 / 128.0)
    pattern = jnp.where(match, factor, 0.0)
    behind = (row & (GROUP - 1)) - (col >> 7)
    lane_half = lax.broadcasted_iota(jnp.int32, (BLOCK, LANES), 1) >> 6

    def two_tiles(n, carry):
        chosen = jnp.where(behind == 2 * n, pattern, 0.0).astype(jnp.bfloat16)
        raised = jnp.dot(lhs[...], chosen, preferred_element_type=jnp.float32).astype(jnp.int32)
        for r in range(replicas):
            for g in range(groups):
                for t in range(2):
                    place = g * GROUP + 2 * n + t
                    dst = meta[r, 0, place]
                    src = meta[r, 1, place]
                    column = jnp.where(src < dst_count, src, src + r * halo_blocks)
                    where = dst * pair_count + (column >> 1)
                    keep = jnp.where(lane_half == (column & 1), 1, 0)
                    first = (r * groups + g) * BLOCK
                    part = raised[first : first + BLOCK, t * LANES : (t + 1) * LANES]
                    blocks[where] += (part & keep).astype(jnp.float32)
        return carry

    lax.fori_loop(0, GROUP // 2, two_tiles, 0)

    def place_row(b, carry):
        rows = pl.ds(pl.multiple_of(b * BLOCK, BLOCK), BLOCK)
        for p in range(pair_count):
            adjacency[rows, p * LANES : (p + 1) * LANES] = blocks[b * pair_count + p].astype(
                jnp.bfloat16
            )
        return carry

    lax.fori_loop(0, dst_count, place_row, 0)


def layer(
    peer_count,
    slots,
    reduce_here,
    adjacency,
    halo,
    meta,
    grad_own,
    grad_core,
    grad_across,
    grad_diagonal,
    feats,
    w_self,
    w_neigh,
    norm,
    out_feats,
    grad_feats,
    weights,
    weight_grad,
    table,
    scale,
    agg,
    grad_pre,
    grad_agg,
    halo_grad,
    halo_out,
    came_halo,
    came_weight,
    summed,
    local_sem,
    halo_send,
    halo_recv,
    part_send,
    part_recv,
    full_send,
    full_recv,
    rep_send,
    rep_recv,
    back_send,
    back_recv,
):
    mine_wide = lax.axis_index("wide")
    mine, core, across, diagonal = partners(4)
    barrier = greet(peer_count, mine_wide, mine, core, across)
    replicas = halo.shape[0]
    node_rows, width = feats.shape
    halo_rows = peer_count * slots
    quarter = node_rows // replicas
    share = width // replicas
    rows = 2 * share // peer_count
    per_half = peer_count // 2

    table[:node_rows, :] = feats[...]
    for r in range(replicas):
        for first in range(0, peer_count, 8):
            start = node_rows + r * halo_rows + first * slots
            table[start : start + 8 * slots, :] = unfolded(halo[r, first : first + 8])
    eye = lax.broadcasted_iota(jnp.int32, (LANES, LANES), 0) == lax.broadcasted_iota(
        jnp.int32, (LANES, LANES), 1
    )
    for n in range(node_rows // LANES):
        counts = norm[n : n + 1, :].astype(jnp.float32)
        column = jnp.sum(jnp.where(eye, counts, 0.0), axis=1, keepdims=True)
        scale[n * LANES : (n + 1) * LANES, :] = lax.rsqrt(column)

    def rows_of(q):
        return pl.ds(pl.multiple_of(q * quarter, quarter), quarter)

    parts = ((mine, grad_own), (core, grad_core), (across, grad_across), (diagonal, grad_diagonal))
    for q, grad_out in parts:
        here = rows_of(q)
        sums = jnp.dot(adjacency[here, :], table[...], preferred_element_type=jnp.float32)
        part_scale = scale[here, :]
        part_agg = (sums * part_scale).astype(jnp.bfloat16)
        agg[here, :] = part_agg
        pre = jnp.dot(feats[here, :], w_self[...], preferred_element_type=jnp.float32) + jnp.dot(
            part_agg, w_neigh[...], preferred_element_type=jnp.float32
        )
        sig = jax.nn.sigmoid(pre)
        if grad_out is grad_own:
            out_feats[...] = (pre * sig).astype(jnp.bfloat16)
        back = (grad_out[...].astype(jnp.float32) * sig * (1.0 + pre * (1.0 - sig))).astype(
            jnp.bfloat16
        )
        grad_pre[here, :] = back
        grad_agg[here, :] = (times_transposed(back, w_neigh[...]) * part_scale).astype(
            jnp.bfloat16
        )

    columns = pl.ds(pl.multiple_of(mine * share, share), share)
    weight_grad[:share, :] = transposed_times(feats[:, columns], grad_pre[...]).astype(
        jnp.bfloat16
    )
    weight_grad[share:, :] = transposed_times(agg[:, columns], grad_pre[...]).astype(jnp.bfloat16)
    pl.semaphore_wait(barrier, peer_count + 1)

    def place(owner_wide, owner_rep):
        start = owner_rep * share + lax.rem(owner_wide, per_half) * rows
        return weights.at[owner_wide // per_half, pl.ds(pl.multiple_of(start, rows), rows)]

    part_copies, halo_copies, full_copies = [], [], []
    if reduce_here:
        for step in range(1, peer_count):
            peer = lax.rem(mine_wide + step, peer_count)
            piece = weight_grad.at[pl.ds(pl.multiple_of(peer * rows, rows), rows)]
            part_copies.append(
                push(
                    piece, came_weight.at[step], part_send.at[step], part_recv.at[step], peer, mine
                )
            )

    block = min(replicas * halo_rows, 512)
    for first in range(0, replicas * halo_rows, block):
        start = node_rows + first
        halo_grad[first : first + block, :] = transposed_times(
            adjacency[:, start : start + block], grad_agg[...]
        )
    for n in range(peer_count):
        start = pl.multiple_of(mine * halo_rows, 8) + n * slots
        halo_out[n] = folded(halo_grad[pl.ds(pl.multiple_of(start, 8), slots), :])
    for step in range(1, peer_count):
        peer = lax.rem(mine_wide + step, peer_count)
        halo_copies.append(
            push(
                halo_out.at[peer],
                came_halo.at[mine, mine_wide],
                halo_send.at[step],
                halo_recv.at[step],
                peer,
                mine,
            )
        )
    kept = pltpu.make_async_copy(
        halo_out.at[mine_wide], came_halo.at[mine, mine_wide], local_sem.at[0]
    )
    kept.start()
    own_rows = rows_of(mine)
    total_grad = transposed_times(adjacency[:, own_rows], grad_agg[...]) + times_transposed(
        grad_pre[own_rows, :], w_self[...]
    )

    if reduce_here:
        total = weight_grad[pl.ds(pl.multiple_of(mine_wide * rows, rows), rows), :].astype(
            jnp.float32
        )
        for step in range(1, peer_count):
            part_copies[step - 1].wait_recv()
            total = total + came_weight[step].astype(jnp.float32)
        summed[...] = total.astype(jnp.bfloat16)
        spot = place(mine_wide, mine)
        for step in range(1, peer_count):
            peer = lax.rem(mine_wide + step, peer_count)
            full_copies.append(
                push(summed, spot, full_send.at[step], full_recv.at[step], peer, mine)
            )
        across_copies = [
            push(summed, spot, rep_send.at[0, 0], rep_recv.at[0, 0], mine_wide, across)
        ]
        core_copies = [push(summed, spot, rep_send.at[1, 0], rep_recv.at[1, 0], mine_wide, core)]
        own_slice = pltpu.make_async_copy(summed, spot, local_sem.at[1])
        own_slice.start()

    kept.wait()
    for copy in halo_copies:
        copy.wait_recv()
    block = came_halo.at[mine]
    back_across = push(block, block, back_send.at[0], back_recv.at[0], mine_wide, across)
    back_core = push(block, block, back_send.at[1], back_recv.at[1], mine_wide, core)

    if reduce_here:
        for step in range(1, peer_count):
            full_copies[step - 1].wait_recv()
            owner = lax.rem(mine_wide + peer_count - step, peer_count)
            spot = place(owner, mine)
            across_copies.append(
                push(spot, spot, rep_send.at[0, step], rep_recv.at[0, step], mine_wide, across)
            )
            core_copies.append(
                push(spot, spot, rep_send.at[1, step], rep_recv.at[1, step], mine_wide, core)
            )

    back_across.wait_recv()
    block = came_halo.at[across]
    back_onward = push(block, block, back_send.at[2], back_recv.at[2], mine_wide, core)
    back_core.wait_recv()
    back_onward.wait_recv()
    for r in range(replicas):
        for first in range(0, peer_count, 8):
            picks = as_column(meta[r, 8 + first : 16 + first, :slots]) - mine * quarter
            chosen = picks == lax.broadcasted_iota(jnp.int32, (8 * slots, quarter), 1)
            total_grad = total_grad + transposed_times(
                jnp.where(chosen, 1.0, 0.0).astype(jnp.bfloat16),
                unfolded(came_halo[r, first : first + 8]),
            )
    grad_feats[...] = total_grad.astype(jnp.bfloat16)

    if reduce_here:
        onward = []
        for step in range(peer_count):
            across_copies[step].wait_recv()
            owner = lax.rem(mine_wide + peer_count - step, peer_count)
            spot = place(owner, across)
            onward.append(
                push(spot, spot, rep_send.at[2, step], rep_recv.at[2, step], mine_wide, core)
            )
        for copy in core_copies + onward:
            copy.wait_recv()
        for copy in part_copies + full_copies + across_copies + core_copies + onward:
            copy.wait_send()
        own_slice.wait()
    for copy in halo_copies + [back_across, back_core, back_onward]:
        copy.wait_send()


def on_device(
    node_feats, w_self, w_neigh, send_rows, tile_dst, tile_src, tile_bits, norm_count, grad_out
):
    node_rows, width = node_feats.shape
    peer_count = lax.axis_size("wide")
    replicas = lax.axis_size("rep")
    slots = send_rows.shape[2]
    tile_total = tile_dst.shape[2]
    quarter = node_rows // replicas
    halo_rows = peer_count * slots
    halo_blocks = halo_rows // BLOCK
    words = tile_bits.reshape(-1, LANES)
    any_spec = pl.BlockSpec(memory_space=pl.ANY)
    vmem_spec = pl.BlockSpec(memory_space=pltpu.VMEM)
    smem_spec = pl.BlockSpec(memory_space=pltpu.SMEM)

    def shaped(dims, held):
        return jax.ShapeDtypeStruct(dims, held)

    def dma(*dims):
        return pltpu.SemaphoreType.DMA(dims)

    by_core = [(n, n + 1 - 2 * (n % 2)) for n in range(replicas)]
    by_chip = [(n, (n + 2) % replicas) for n in range(replicas)]
    grad_across = lax.ppermute(grad_out, "rep", by_chip)
    grad_core = lax.ppermute(grad_out, "rep", by_core)
    grad_diagonal = lax.ppermute(grad_across, "rep", by_core)

    halo_shape = (replicas, peer_count, 2 * slots, width // 2)
    meta_shape = (8 + peer_count, tile_total)
    with jax.named_scope("spread_inputs"):
        all_bits, all_meta, all_halo = pl.pallas_call(
            functools.partial(spread_inputs, peer_count, slots),
            out_shape=(
                shaped((replicas,) + words.shape, jnp.int32),
                shaped((replicas,) + meta_shape, jnp.int32),
                shaped(halo_shape, jnp.bfloat16),
            ),
            in_specs=[vmem_spec] * 5,
            out_specs=(any_spec,) * 3,
            scratch_shapes=[
                pltpu.VMEM(words.shape, jnp.int32),
                pltpu.VMEM(meta_shape, jnp.int32),
                pltpu.VMEM(halo_shape[1:], jnp.bfloat16),
                dma(3),
                dma(9),
                dma(9),
                dma(peer_count),
                dma(peer_count),
            ],
            compiler_params=pltpu.CompilerParams(
                collective_id=0, has_side_effects=True, vmem_limit_bytes=VMEM_BYTES
            ),
        )(words, tile_dst[0], tile_src[0], send_rows[0], node_feats)

    columns = node_rows + replicas * halo_rows
    pair_count = columns // LANES
    dst_count = node_rows // BLOCK
    with jax.named_scope("build_adjacency"):
        adjacency = pl.pallas_call(
            functools.partial(build_adjacency, dst_count, halo_blocks),
            out_shape=shaped((node_rows, columns), jnp.bfloat16),
            in_specs=[smem_spec, vmem_spec],
            out_specs=vmem_spec,
            scratch_shapes=[
                pltpu.VMEM((dst_count * pair_count, BLOCK, LANES), jnp.float32),
                pltpu.VMEM((replicas * words.shape[0], 2 * LANES), jnp.bfloat16),
            ],
            compiler_params=pltpu.CompilerParams(vmem_limit_bytes=VMEM_BYTES),
            cost_estimate=pl.CostEstimate(
                flops=8 * 10**9, bytes_accessed=4 * 10**6, transcendentals=0
            ),
        )(all_meta, all_bits)

    rows = 2 * width // replicas // peer_count
    reduce_here = rows % 16 == 0
    piece = (rows if reduce_here else 16, width)
    with jax.named_scope("layer"):
        out_feats, grad_feats, weights, weight_grad = pl.pallas_call(
            functools.partial(layer, peer_count, slots, reduce_here),
            out_shape=(
                shaped((quarter, width), jnp.bfloat16),
                shaped((quarter, width), jnp.bfloat16),
                shaped((2, width, width), jnp.bfloat16),
                shaped((2 * width // replicas, width), jnp.bfloat16),
            ),
            in_specs=[vmem_spec] * 11,
            out_specs=(vmem_spec, vmem_spec, any_spec, vmem_spec),
            scratch_shapes=[
                pltpu.VMEM((columns, width), jnp.bfloat16),
                pltpu.VMEM((node_rows, 1), jnp.float32),
                pltpu.VMEM((node_rows, width), jnp.bfloat16),
                pltpu.VMEM((node_rows, width), jnp.bfloat16),
                pltpu.VMEM((node_rows, width), jnp.bfloat16),
                pltpu.VMEM((replicas * halo_rows, width), jnp.float32),
                pltpu.VMEM(halo_shape[1:], jnp.bfloat16),
                pltpu.VMEM(halo_shape, jnp.bfloat16),
                pltpu.VMEM((peer_count,) + piece, jnp.bfloat16),
                pltpu.VMEM(piece, jnp.bfloat16),
                dma(2),
            ]
            + [dma(peer_count)] * 6
            + [dma(3, peer_count)] * 2
            + [dma(3)] * 2,
            compiler_params=pltpu.CompilerParams(
                collective_id=1, has_side_effects=True, vmem_limit_bytes=VMEM_BYTES
            ),
        )(
            adjacency,
            all_halo,
            all_meta,
            grad_out,
            grad_core,
            grad_across,
            grad_diagonal,
            node_feats,
            w_self,
            w_neigh,
            norm_count.reshape(-1, LANES),
        )
    if reduce_here:
        return out_feats, grad_feats, weights[0], weights[1]
    total = lax.psum(weight_grad.astype(jnp.float32), "wide").astype(jnp.bfloat16)
    whole = lax.all_gather(total, "rep", axis=0, tiled=False)
    share = width // replicas
    return (
        out_feats,
        grad_feats,
        whole[:, :share].reshape(width, width),
        whole[:, share:].reshape(width, width),
    )


def solution(mesh):
    in_specs = (
        P("wide", None),
        P(),
        P(),
        P("wide", None, "rep"),
        P("wide", "rep", None),
        P("wide", "rep", None),
        P("wide", "rep", None),
        P("wide"),
        P(("wide", "rep"), None),
    )
    out_specs = (P(("wide", "rep"), None), P(("wide", "rep"), None), P(), P())
    return jax.shard_map(
        on_device, mesh=mesh, in_specs=in_specs, out_specs=out_specs, check_vma=False
    )
```

```python
import functools

import jax
import jax.numpy as jnp
from jax import lax
from jax.experimental import pallas as pl
from jax.experimental.pallas import tpu as pltpu
from jax.sharding import PartitionSpec as P

BLOCK = 64
GROUP = 32
LANES = 128
MESH = pl.DeviceIdType.MESH
VMEM_BYTES = 56 * 1024 * 1024


def partners(replicas):
    mine = lax.axis_index("rep")
    core = mine + 1 - 2 * lax.rem(mine, 2)
    across = lax.rem(mine + 2, replicas)
    diagonal = lax.rem(core + 2, replicas)
    return mine, core, across, diagonal


def times_transposed(left, right):
    return lax.dot_general(
        left, right, (((1,), (1,)), ((), ())), preferred_element_type=jnp.float32
    )


def transposed_times(left, right):
    return lax.dot_general(
        left, right, (((0,), (0,)), ((), ())), preferred_element_type=jnp.float32
    )


def as_column(picks):
    count, slots = picks.shape
    same = lax.broadcasted_iota(jnp.int32, (count, slots, slots), 1) == lax.broadcasted_iota(
        jnp.int32, (count, slots, slots), 2
    )
    wide = jnp.broadcast_to(picks.astype(jnp.float32)[:, None, :], (count, slots, slots))
    column = jnp.sum(jnp.where(same, wide, 0.0), axis=2, keepdims=True)
    return column.reshape(count * slots, 1).astype(jnp.int32)


def folded(part):
    half = part.shape[1] // 2
    return jnp.concatenate([part[:, :half], part[:, half:]], axis=0).astype(jnp.bfloat16)


def unfolded(parts):
    count, rows, half = parts.shape
    wide = parts.astype(jnp.float32)
    joined = jnp.concatenate([wide[:, : rows // 2, :], wide[:, rows // 2 :, :]], axis=2)
    return joined.reshape(count * rows // 2, 2 * half).astype(jnp.bfloat16)


def sort_words(words, sorted_words):
    rows = lax.broadcasted_iota(jnp.int32, (LANES, LANES), 0)
    lanes = lax.broadcasted_iota(jnp.int32, (LANES, LANES), 1)
    wanted = (rows // GROUP) == lanes % 4
    pick_row = lax.broadcasted_iota(jnp.int32, (GROUP, 2 * LANES), 0)
    pick_lane = lax.broadcasted_iota(jnp.int32, (GROUP, 2 * LANES), 1) % LANES
    pick = jnp.where(pick_row == pick_lane // 4, 1.0, 0.0).astype(jnp.bfloat16)
    for group in range(words.shape[0] // BLOCK):
        for h in range(2):
            part = words[pl.ds(group * BLOCK + h, GROUP, stride=2), :]
            low = (part & 255).astype(jnp.float32)
            high = (part - (part & 255)).astype(jnp.float32)
            both = jnp.concatenate(
                [
                    jnp.where(wanted, jnp.concatenate([half] * 4, axis=0), 0.0)
                    for half in (low, high)
                ],
                axis=1,
            ).astype(jnp.bfloat16)
            start = group * BLOCK + h * GROUP
            sorted_words[start : start + GROUP, :] = times_transposed(pick, both).astype(jnp.int32)


def greet(peer_count, mine_wide, mine, core, across):
    barrier = pltpu.get_barrier_semaphore()
    for step in range(1, peer_count):
        peer = lax.rem(mine_wide + step, peer_count)
        pl.semaphore_signal(barrier, inc=1, device_id=(peer, mine), device_id_type=MESH)
    for other in (core, across):
        pl.semaphore_signal(barrier, inc=1, device_id=(mine_wide, other), device_id_type=MESH)
    return barrier


def push(src, dst, send, recv, wide_to, rep_to):
    copy = pltpu.make_async_remote_copy(
        src_ref=src,
        dst_ref=dst,
        send_sem=send,
        recv_sem=recv,
        device_id=(wide_to, rep_to),
        device_id_type=MESH,
    )
    copy.start()
    return copy


def spread_inputs(
    peer_count,
    slots,
    words,
    tile_dst,
    tile_src,
    send_rows,
    feats,
    all_bits,
    all_meta,
    halo,
    bits,
    meta,
    outgoing,
    local_sem,
    send_sem,
    recv_sem,
    halo_send,
    halo_recv,
):
    mine_wide = lax.axis_index("wide")
    mine, core, across, diagonal = partners(4)
    barrier = greet(peer_count, mine_wide, mine, core, across)
    meta[...] = jnp.zeros_like(meta)
    meta[0:1, :] = tile_dst[...]
    meta[1:2, :] = tile_src[...]
    meta[8:, :slots] = send_rows[...]
    node_rows = feats.shape[0]
    for first in range(0, peer_count, 8):
        picks = as_column(send_rows[first : first + 8, :])
        chosen = picks == lax.broadcasted_iota(jnp.int32, (8 * slots, node_rows), 1)
        rows = jnp.dot(
            jnp.where(chosen, 1.0, 0.0).astype(jnp.bfloat16),
            feats[...],
            preferred_element_type=jnp.float32,
        )
        for n in range(8):
            outgoing[first + n] = folded(rows[n * slots : (n + 1) * slots])
    sort_words(words, bits)
    pl.semaphore_wait(barrier, peer_count + 1)

    exchange = []
    for step in range(1, peer_count):
        peer = lax.rem(mine_wide + step, peer_count)
        exchange.append(
            push(
                outgoing.at[peer],
                halo.at[mine_wide],
                halo_send.at[step],
                halo_recv.at[step],
                peer,
                mine,
            )
        )
    pairs = ((bits, all_bits), (meta, all_meta))
    to_across = [
        push(src, dst.at[mine], send_sem.at[n], recv_sem.at[n], mine_wide, across)
        for n, (src, dst) in enumerate(pairs)
    ]
    to_core = [
        push(src, dst.at[mine], send_sem.at[3 + n], recv_sem.at[3 + n], mine_wide, core)
        for n, (src, dst) in enumerate(pairs)
    ]
    own = [
        pltpu.make_async_copy(src, dst.at[mine], local_sem.at[n])
        for n, (src, dst) in enumerate(pairs)
    ]
    own.append(
        pltpu.make_async_copy(outgoing.at[mine_wide], halo.at[mine_wide], local_sem.at[2])
    )
    for copy in own:
        copy.start()
    onward = []
    for n, dst in enumerate((all_bits, all_meta)):
        to_across[n].wait_recv()
        block = dst.at[across]
        onward.append(push(block, block, send_sem.at[6 + n], recv_sem.at[6 + n], mine_wide, core))
    for copy in to_core + onward + exchange:
        copy.wait_recv()
    for copy in to_across + to_core + onward + exchange:
        copy.wait_send()
    for copy in own:
        copy.wait()


def build_adjacency(
    dst_count, halo_blocks, meta, bits, adjacency, low_sum, high_sum, lhs, raised_even, raised_odd
):
    replicas = bits.shape[0]
    per_sum = replicas // 2
    own_pairs = dst_count // 2
    halo_pairs = per_sum * halo_blocks // 2
    pair_count = own_pairs + halo_pairs
    groups = bits.shape[1] // BLOCK
    sums = (low_sum, high_sum)

    for target in sums:
        target[...] = jnp.zeros_like(target)
    for r in range(replicas):
        words = bits[r]
        rows = pl.ds(r * words.shape[0], words.shape[0])
        lhs[rows, :LANES] = (words & 255).astype(jnp.float32).astype(jnp.bfloat16)
        lhs[rows, LANES:] = (words >> 8).astype(jnp.float32).astype(jnp.bfloat16)

    row = lax.broadcasted_iota(jnp.int32, (2 * LANES, 2 * LANES), 0)
    col = lax.broadcasted_iota(jnp.int32, (2 * LANES, 2 * LANES), 1)
    bit = col & (BLOCK - 1)
    match = (((row >> 5) & 3) == (bit >> 4)) & ((row >> 7) == ((bit >> 3) & 1))
    factor = (1 << (7 - (bit & 7))).astype(jnp.float32) * (1.0 / 128.0)
    pattern = jnp.where(match, factor, 0.0)
    behind = (row & (GROUP - 1)) - (col >> 7)
    lane_half = lax.broadcasted_iota(jnp.int32, (BLOCK, LANES), 1) >> 6

    def expand(n):
        chosen = jnp.where(behind == 2 * n, pattern, 0.0).astype(jnp.bfloat16)
        return jnp.dot(lhs[...], chosen, preferred_element_type=jnp.float32)

    def add_tiles(raised, n):
        for g in range(groups):
            for t in range(2):
                for turn in range(replicas):
                    r = (turn % 2) * per_sum + turn // 2
                    place = g * GROUP + 2 * n + t
                    dst = meta[r, 0, place]
                    src = meta[r, 1, place]
                    column = jnp.where(src < dst_count, src, src + (r % per_sum) * halo_blocks)
                    where = dst * pair_count + (column >> 1)
                    keep = jnp.where(lane_half == (column & 1), 1, 0)
                    first = (r * groups + g) * BLOCK
                    part = raised[first : first + BLOCK, t * LANES : (t + 1) * LANES]
                    sums[r // per_sum][where] += (
                        (part.astype(jnp.int32) & keep).astype(jnp.float32).astype(jnp.bfloat16)
                    )

    raised_even[...] = expand(0)

    def four_tiles(m, carry):
        raised_odd[...] = expand(2 * m + 1)
        add_tiles(raised_even, 2 * m)
        raised_even[...] = expand(2 * m + 2)
        add_tiles(raised_odd, 2 * m + 1)
        return carry

    lax.fori_loop(0, GROUP // 4, four_tiles, 0)

    def place_row(b, carry):
        rows = pl.ds(pl.multiple_of(b * BLOCK, BLOCK), BLOCK)
        for p in range(own_pairs):
            both = low_sum[b * pair_count + p].astype(jnp.float32) + high_sum[
                b * pair_count + p
            ].astype(jnp.float32)
            adjacency[rows, p * LANES : (p + 1) * LANES] = both.astype(jnp.bfloat16)
        for n, target in enumerate(sums):
            for p in range(halo_pairs):
                start = (own_pairs + n * halo_pairs + p) * LANES
                adjacency[rows, start : start + LANES] = target[b * pair_count + own_pairs + p]
        return carry

    lax.fori_loop(0, dst_count, place_row, 0)


def layer(
    peer_count,
    slots,
    reduce_here,
    adjacency,
    halo_own,
    halo_core,
    halo_across,
    halo_diagonal,
    meta,
    grad_own,
    grad_core,
    grad_across,
    grad_diagonal,
    feats,
    w_self,
    w_neigh,
    norm,
    out_feats,
    grad_feats,
    weights,
    weight_grad,
    table,
    scale,
    agg,
    grad_pre,
    grad_agg,
    halo_grad,
    halo_out,
    came_halo,
    came_weight,
    summed,
    local_sem,
    halo_send,
    halo_recv,
    part_send,
    part_recv,
    full_send,
    full_recv,
    rep_send,
    rep_recv,
    back_send,
    back_recv,
):
    mine_wide = lax.axis_index("wide")
    mine, core, across, diagonal = partners(4)
    barrier = greet(peer_count, mine_wide, mine, core, across)
    replicas = meta.shape[0]
    node_rows, width = feats.shape
    halo_rows = peer_count * slots
    quarter = node_rows // replicas
    share = width // replicas
    rows = 2 * share // peer_count
    per_half = peer_count // 2

    table[:node_rows, :] = feats[...]
    halos = ((mine, halo_own), (core, halo_core), (across, halo_across), (diagonal, halo_diagonal))
    for r, halo in halos:
        for first in range(0, peer_count, 8):
            start = pl.multiple_of(node_rows + r * halo_rows + first * slots, 8 * slots)
            table[pl.ds(start, 8 * slots), :] = unfolded(halo[first : first + 8])
    eye = lax.broadcasted_iota(jnp.int32, (LANES, LANES), 0) == lax.broadcasted_iota(
        jnp.int32, (LANES, LANES), 1
    )
    for n in range(node_rows // LANES):
        counts = norm[n : n + 1, :].astype(jnp.float32)
        column = jnp.sum(jnp.where(eye, counts, 0.0), axis=1, keepdims=True)
        scale[n * LANES : (n + 1) * LANES, :] = lax.rsqrt(column)

    def rows_of(q):
        return pl.ds(pl.multiple_of(q * quarter, quarter), quarter)

    parts = ((mine, grad_own), (core, grad_core), (across, grad_across), (diagonal, grad_diagonal))
    for q, grad_out in parts:
        here = rows_of(q)
        sums = jnp.dot(adjacency[here, :], table[...], preferred_element_type=jnp.float32)
        part_scale = scale[here, :]
        part_agg = (sums * part_scale).astype(jnp.bfloat16)
        agg[here, :] = part_agg
        pre = jnp.dot(feats[here, :], w_self[...], preferred_element_type=jnp.float32) + jnp.dot(
            part_agg, w_neigh[...], preferred_element_type=jnp.float32
        )
        sig = jax.nn.sigmoid(pre)
        if grad_out is grad_own:
            out_feats[...] = (pre * sig).astype(jnp.bfloat16)
        back = (grad_out[...].astype(jnp.float32) * sig * (1.0 + pre * (1.0 - sig))).astype(
            jnp.bfloat16
        )
        grad_pre[here, :] = back
        grad_agg[here, :] = (times_transposed(back, w_neigh[...]) * part_scale).astype(
            jnp.bfloat16
        )

    columns = pl.ds(pl.multiple_of(mine * share, share), share)
    weight_grad[:share, :] = transposed_times(feats[:, columns], grad_pre[...]).astype(
        jnp.bfloat16
    )
    weight_grad[share:, :] = transposed_times(agg[:, columns], grad_pre[...]).astype(jnp.bfloat16)
    pl.semaphore_wait(barrier, peer_count + 1)

    def place(owner_wide, owner_rep):
        start = owner_rep * share + lax.rem(owner_wide, per_half) * rows
        return weights.at[owner_wide // per_half, pl.ds(pl.multiple_of(start, rows), rows)]

    part_copies, halo_copies = [], []
    if reduce_here:
        for step in range(1, peer_count):
            peer = lax.rem(mine_wide + step, peer_count)
            piece = weight_grad.at[pl.ds(pl.multiple_of(peer * rows, rows), rows)]
            part_copies.append(
                push(
                    piece, came_weight.at[step], part_send.at[step], part_recv.at[step], peer, mine
                )
            )

    block = min(replicas * halo_rows, 512)
    for first in range(0, replicas * halo_rows, block):
        start = node_rows + first
        halo_grad[first : first + block, :] = transposed_times(
            adjacency[:, start : start + block], grad_agg[...]
        )
    for n in range(peer_count):
        start = pl.multiple_of(mine * halo_rows, 8) + n * slots
        halo_out[n] = folded(halo_grad[pl.ds(pl.multiple_of(start, 8), slots), :])
    for step in range(1, peer_count):
        peer = lax.rem(mine_wide + step, peer_count)
        halo_copies.append(
            push(
                halo_out.at[peer],
                came_halo.at[mine, mine_wide],
                halo_send.at[step],
                halo_recv.at[step],
                peer,
                mine,
            )
        )
    kept = pltpu.make_async_copy(
        halo_out.at[mine_wide], came_halo.at[mine, mine_wide], local_sem.at[0]
    )
    kept.start()
    own_rows = rows_of(mine)
    total_grad = transposed_times(adjacency[:, own_rows], grad_agg[...]) + times_transposed(
        grad_pre[own_rows, :], w_self[...]
    )

    if reduce_here:
        total = weight_grad[pl.ds(pl.multiple_of(mine_wide * rows, rows), rows), :].astype(
            jnp.float32
        )
        for step in range(1, peer_count):
            part_copies[step - 1].wait_recv()
            total = total + came_weight[step].astype(jnp.float32)
        summed[...] = total.astype(jnp.bfloat16)
        spot = place(mine_wide, mine)
        beside = mine_wide + 1 - 2 * lax.rem(mine_wide, 2)
        hops = list(range(1, per_half))
        full_copies = {}
        across_copies, core_copies = {}, {}

        def share_piece(slot, src, dst):
            across_copies[slot] = push(
                src, dst, rep_send.at[0, slot], rep_recv.at[0, slot], mine_wide, across
            )
            core_copies[slot] = push(
                src, dst, rep_send.at[1, slot], rep_recv.at[1, slot], mine_wide, core
            )

        def owner_of(slot):
            base = mine_wide if slot < per_half else beside
            return lax.rem(base + peer_count - 2 * (slot % per_half), peer_count)

        full_copies[per_half] = push(
            summed, spot, full_send.at[per_half], full_recv.at[per_half], beside, mine
        )
        share_piece(0, summed, spot)
        for hop in hops:
            peer = lax.rem(mine_wide + 2 * hop, peer_count)
            full_copies[hop] = push(
                summed, spot, full_send.at[hop], full_recv.at[hop], peer, mine
            )
        own_slice = pltpu.make_async_copy(summed, spot, local_sem.at[1])
        own_slice.start()

    kept.wait()
    for copy in halo_copies:
        copy.wait_recv()
    block = came_halo.at[mine]
    back_across = push(block, block, back_send.at[0], back_recv.at[0], mine_wide, across)
    back_core = push(block, block, back_send.at[1], back_recv.at[1], mine_wide, core)

    if reduce_here:
        order = [per_half] + sorted(hops, key=lambda hop: min(hop, per_half - hop))
        order = order + [per_half + hop for hop in order[1:]]
        for slot in order:
            full_copies[slot].wait_recv()
            spot = place(owner_of(slot), mine)
            if slot < per_half:
                ahead = per_half + slot
                full_copies[ahead] = push(
                    spot, spot, full_send.at[ahead], full_recv.at[ahead], beside, mine
                )
            share_piece(slot, spot, spot)

    back_across.wait_recv()
    block = came_halo.at[across]
    back_onward = push(block, block, back_send.at[2], back_recv.at[2], mine_wide, core)
    back_core.wait_recv()
    back_onward.wait_recv()
    for r in range(replicas):
        for first in range(0, peer_count, 8):
            picks = as_column(meta[r, 8 + first : 16 + first, :slots]) - mine * quarter
            chosen = picks == lax.broadcasted_iota(jnp.int32, (8 * slots, quarter), 1)
            total_grad = total_grad + transposed_times(
                jnp.where(chosen, 1.0, 0.0).astype(jnp.bfloat16),
                unfolded(came_halo[r, first : first + 8]),
            )
    grad_feats[...] = total_grad.astype(jnp.bfloat16)

    if reduce_here:
        onward = []
        for slot in [0] + order:
            across_copies[slot].wait_recv()
            spot = place(owner_of(slot), across)
            onward.append(
                push(spot, spot, rep_send.at[2, slot], rep_recv.at[2, slot], mine_wide, core)
            )
        sent = list(full_copies.values()) + list(across_copies.values())
        sent = sent + list(core_copies.values()) + onward
        for copy in list(core_copies.values()) + onward:
            copy.wait_recv()
        for copy in part_copies + sent:
            copy.wait_send()
        own_slice.wait()
    for copy in halo_copies + [back_across, back_core, back_onward]:
        copy.wait_send()


def deliver(out_feats, grad_feats, weights, out_to, grad_to, self_to, neigh_to, sems):
    pairs = (
        (out_feats, out_to),
        (grad_feats, grad_to),
        (weights.at[0], self_to),
        (weights.at[1], neigh_to),
    )
    copies = [pltpu.make_async_copy(src, dst, sems.at[n]) for n, (src, dst) in enumerate(pairs)]
    for copy in copies:
        copy.start()
    for copy in copies:
        copy.wait()


def on_device(
    node_feats, w_self, w_neigh, send_rows, tile_dst, tile_src, tile_bits, norm_count, grad_out
):
    node_rows, width = node_feats.shape
    peer_count = lax.axis_size("wide")
    replicas = lax.axis_size("rep")
    slots = send_rows.shape[2]
    tile_total = tile_dst.shape[2]
    quarter = node_rows // replicas
    halo_rows = peer_count * slots
    halo_blocks = halo_rows // BLOCK
    words = tile_bits.reshape(-1, LANES)
    any_spec = pl.BlockSpec(memory_space=pl.ANY)
    vmem_spec = pl.BlockSpec(memory_space=pltpu.VMEM)
    smem_spec = pl.BlockSpec(memory_space=pltpu.SMEM)

    def shaped(dims, held):
        return jax.ShapeDtypeStruct(dims, held)

    def dma(*dims):
        return pltpu.SemaphoreType.DMA(dims)

    by_core = [(n, n + 1 - 2 * (n % 2)) for n in range(replicas)]
    by_chip = [(n, (n + 2) % replicas) for n in range(replicas)]
    grad_across = lax.ppermute(grad_out, "rep", by_chip)
    grad_core = lax.ppermute(grad_out, "rep", by_core)
    grad_diagonal = lax.ppermute(grad_across, "rep", by_core)

    halo_shape = (replicas, peer_count, 2 * slots, width // 2)
    meta_shape = (8 + peer_count, tile_total)
    with jax.named_scope("spread_inputs"):
        all_bits, all_meta, halo = pl.pallas_call(
            functools.partial(spread_inputs, peer_count, slots),
            out_shape=(
                shaped((replicas,) + words.shape, jnp.int32),
                shaped((replicas,) + meta_shape, jnp.int32),
                shaped(halo_shape[1:], jnp.bfloat16),
            ),
            in_specs=[vmem_spec] * 5,
            out_specs=(any_spec,) * 3,
            scratch_shapes=[
                pltpu.VMEM(words.shape, jnp.int32),
                pltpu.VMEM(meta_shape, jnp.int32),
                pltpu.VMEM(halo_shape[1:], jnp.bfloat16),
                dma(3),
                dma(9),
                dma(9),
                dma(peer_count),
                dma(peer_count),
            ],
            compiler_params=pltpu.CompilerParams(
                collective_id=0, has_side_effects=True, vmem_limit_bytes=VMEM_BYTES
            ),
        )(words, tile_dst[0], tile_src[0], send_rows[0], node_feats)

    halo_across = lax.ppermute(halo, "rep", by_chip)
    halo_core = lax.ppermute(halo, "rep", by_core)
    halo_diagonal = lax.ppermute(halo_across, "rep", by_core)

    columns = node_rows + replicas * halo_rows
    dst_count = node_rows // BLOCK
    sum_shape = (dst_count * (dst_count + replicas // 2 * halo_blocks) // 2, BLOCK, LANES)
    with jax.named_scope("build_adjacency"):
        adjacency = pl.pallas_call(
            functools.partial(build_adjacency, dst_count, halo_blocks),
            out_shape=shaped((node_rows, columns), jnp.bfloat16),
            in_specs=[smem_spec, vmem_spec],
            out_specs=vmem_spec,
            scratch_shapes=[
                pltpu.VMEM(sum_shape, jnp.bfloat16),
                pltpu.VMEM(sum_shape, jnp.bfloat16),
                pltpu.VMEM((replicas * words.shape[0], 2 * LANES), jnp.bfloat16),
                pltpu.VMEM((replicas * words.shape[0], 2 * LANES), jnp.float32),
                pltpu.VMEM((replicas * words.shape[0], 2 * LANES), jnp.float32),
            ],
            compiler_params=pltpu.CompilerParams(vmem_limit_bytes=VMEM_BYTES),
            cost_estimate=pl.CostEstimate(
                flops=8 * 10**9, bytes_accessed=4 * 10**6, transcendentals=0
            ),
        )(all_meta, all_bits)

    rows = 2 * width // replicas // peer_count
    reduce_here = rows % 16 == 0
    piece = (rows if reduce_here else 16, width)
    with jax.named_scope("layer"):
        out_feats, grad_feats, weights, weight_grad = pl.pallas_call(
            functools.partial(layer, peer_count, slots, reduce_here),
            out_shape=(
                shaped((quarter, width), jnp.bfloat16),
                shaped((quarter, width), jnp.bfloat16),
                shaped((2, width, width), jnp.bfloat16),
                shaped((2 * width // replicas, width), jnp.bfloat16),
            ),
            in_specs=[vmem_spec] * 14,
            out_specs=(vmem_spec, vmem_spec, any_spec, vmem_spec),
            scratch_shapes=[
                pltpu.VMEM((columns, width), jnp.bfloat16),
                pltpu.VMEM((node_rows, 1), jnp.float32),
                pltpu.VMEM((node_rows, width), jnp.bfloat16),
                pltpu.VMEM((node_rows, width), jnp.bfloat16),
                pltpu.VMEM((node_rows, width), jnp.bfloat16),
                pltpu.VMEM((replicas * halo_rows, width), jnp.float32),
                pltpu.VMEM(halo_shape[1:], jnp.bfloat16),
                pltpu.VMEM(halo_shape, jnp.bfloat16),
                pltpu.VMEM((peer_count,) + piece, jnp.bfloat16),
                pltpu.VMEM(piece, jnp.bfloat16),
                dma(2),
            ]
            + [dma(peer_count)] * 6
            + [dma(3, peer_count)] * 2
            + [dma(3)] * 2,
            compiler_params=pltpu.CompilerParams(
                collective_id=1, has_side_effects=True, vmem_limit_bytes=VMEM_BYTES
            ),
        )(
            adjacency,
            halo,
            halo_core,
            halo_across,
            halo_diagonal,
            all_meta,
            grad_out,
            grad_core,
            grad_across,
            grad_diagonal,
            node_feats,
            w_self,
            w_neigh,
            norm_count.reshape(-1, LANES),
        )
    if reduce_here:
        with jax.named_scope("deliver"):
            return pl.pallas_call(
                deliver,
                out_shape=(
                    shaped((quarter, width), jnp.bfloat16),
                    shaped((quarter, width), jnp.bfloat16),
                    shaped((width, width), jnp.bfloat16),
                    shaped((width, width), jnp.bfloat16),
                ),
                in_specs=[vmem_spec] * 3,
                out_specs=(any_spec,) * 4,
                scratch_shapes=[dma(4)],
            )(out_feats, grad_feats, weights)
    total = lax.psum(weight_grad.astype(jnp.float32), "wide").astype(jnp.bfloat16)
    whole = lax.all_gather(total, "rep", axis=0, tiled=False)
    share = width // replicas
    return (
        out_feats,
        grad_feats,
        whole[:, :share].reshape(width, width),
        whole[:, share:].reshape(width, width),
    )


def solution(mesh):
    in_specs = (
        P("wide", None),
        P(),
        P(),
        P("wide", None, "rep"),
        P("wide", "rep", None),
        P("wide", "rep", None),
        P("wide", "rep", None),
        P("wide"),
        P(("wide", "rep"), None),
    )
    out_specs = (P(("wide", "rep"), None), P(("wide", "rep"), None), P(), P())
    return jax.shard_map(
        on_device, mesh=mesh, in_specs=in_specs, out_specs=out_specs, check_vma=False
    )
```

```python
import functools

import jax
import jax.numpy as jnp
from jax import lax
from jax.experimental import pallas as pl
from jax.experimental.pallas import tpu as pltpu
from jax.sharding import PartitionSpec as P

BLOCK = 64
GROUP = 32
LANES = 128
MESH = pl.DeviceIdType.MESH
VMEM_BYTES = 56 * 1024 * 1024


def partners(replicas):
    mine = lax.axis_index("rep")
    core = mine + 1 - 2 * lax.rem(mine, 2)
    across = lax.rem(mine + 2, replicas)
    diagonal = lax.rem(core + 2, replicas)
    return mine, core, across, diagonal


def times_transposed(left, right):
    return lax.dot_general(
        left, right, (((1,), (1,)), ((), ())), preferred_element_type=jnp.float32
    )


def transposed_times(left, right):
    return lax.dot_general(
        left, right, (((0,), (0,)), ((), ())), preferred_element_type=jnp.float32
    )


def as_column(picks):
    count, slots = picks.shape
    same = lax.broadcasted_iota(jnp.int32, (count, slots, slots), 1) == lax.broadcasted_iota(
        jnp.int32, (count, slots, slots), 2
    )
    wide = jnp.broadcast_to(picks.astype(jnp.float32)[:, None, :], (count, slots, slots))
    column = jnp.sum(jnp.where(same, wide, 0.0), axis=2, keepdims=True)
    return column.reshape(count * slots, 1).astype(jnp.int32)


def folded(part):
    half = part.shape[1] // 2
    return jnp.concatenate([part[:, :half], part[:, half:]], axis=0).astype(jnp.bfloat16)


def unfolded(parts):
    count, rows, half = parts.shape
    wide = parts.astype(jnp.float32)
    joined = jnp.concatenate([wide[:, : rows // 2, :], wide[:, rows // 2 :, :]], axis=2)
    return joined.reshape(count * rows // 2, 2 * half).astype(jnp.bfloat16)


def sort_words(words, sorted_words):
    rows = lax.broadcasted_iota(jnp.int32, (LANES, LANES), 0)
    lanes = lax.broadcasted_iota(jnp.int32, (LANES, LANES), 1)
    wanted = (rows // GROUP) == lanes % 4
    pick_row = lax.broadcasted_iota(jnp.int32, (GROUP, 2 * LANES), 0)
    pick_lane = lax.broadcasted_iota(jnp.int32, (GROUP, 2 * LANES), 1) % LANES
    pick = jnp.where(pick_row == pick_lane // 4, 1.0, 0.0).astype(jnp.bfloat16)
    for group in range(words.shape[0] // BLOCK):
        for h in range(2):
            part = words[pl.ds(group * BLOCK + h, GROUP, stride=2), :]
            low = (part & 255).astype(jnp.float32)
            high = (part - (part & 255)).astype(jnp.float32)
            both = jnp.concatenate(
                [
                    jnp.where(wanted, jnp.concatenate([half] * 4, axis=0), 0.0)
                    for half in (low, high)
                ],
                axis=1,
            ).astype(jnp.bfloat16)
            start = group * BLOCK + h * GROUP
            sorted_words[start : start + GROUP, :] = times_transposed(pick, both).astype(jnp.int32)


def greet(peer_count, mine_wide, mine, core, across):
    barrier = pltpu.get_barrier_semaphore()
    for step in range(1, peer_count):
        peer = lax.rem(mine_wide + step, peer_count)
        pl.semaphore_signal(barrier, inc=1, device_id=(peer, mine), device_id_type=MESH)
    for other in (core, across):
        pl.semaphore_signal(barrier, inc=1, device_id=(mine_wide, other), device_id_type=MESH)
    return barrier


def push(src, dst, send, recv, wide_to, rep_to):
    copy = pltpu.make_async_remote_copy(
        src_ref=src,
        dst_ref=dst,
        send_sem=send,
        recv_sem=recv,
        device_id=(wide_to, rep_to),
        device_id_type=MESH,
    )
    copy.start()
    return copy


def spread_inputs(
    peer_count,
    slots,
    words,
    tile_dst,
    tile_src,
    send_rows,
    feats,
    all_bits,
    all_meta,
    all_halo,
    bits,
    meta,
    outgoing,
    local_sem,
    send_sem,
    recv_sem,
    halo_send,
    halo_recv,
):
    mine_wide = lax.axis_index("wide")
    mine, core, across, diagonal = partners(4)
    barrier = greet(peer_count, mine_wide, mine, core, across)
    meta[...] = jnp.zeros_like(meta)
    meta[0:1, :] = tile_dst[...]
    meta[1:2, :] = tile_src[...]
    meta[8:, :slots] = send_rows[...]
    node_rows = feats.shape[0]
    for first in range(0, peer_count, 8):
        picks = as_column(send_rows[first : first + 8, :])
        chosen = picks == lax.broadcasted_iota(jnp.int32, (8 * slots, node_rows), 1)
        rows = jnp.dot(
            jnp.where(chosen, 1.0, 0.0).astype(jnp.bfloat16),
            feats[...],
            preferred_element_type=jnp.float32,
        )
        for n in range(8):
            outgoing[first + n] = folded(rows[n * slots : (n + 1) * slots])
    sort_words(words, bits)
    pl.semaphore_wait(barrier, peer_count + 1)

    exchange = []
    for step in range(1, peer_count):
        peer = lax.rem(mine_wide + step, peer_count)
        exchange.append(
            push(
                outgoing.at[peer],
                all_halo.at[mine, mine_wide],
                halo_send.at[step],
                halo_recv.at[step],
                peer,
                mine,
            )
        )
    pairs = ((bits, all_bits), (meta, all_meta))
    to_across = [
        push(src, dst.at[mine], send_sem.at[n], recv_sem.at[n], mine_wide, across)
        for n, (src, dst) in enumerate(pairs)
    ]
    to_core = [
        push(src, dst.at[mine], send_sem.at[3 + n], recv_sem.at[3 + n], mine_wide, core)
        for n, (src, dst) in enumerate(pairs)
    ]
    own = [
        pltpu.make_async_copy(src, dst.at[mine], local_sem.at[n])
        for n, (src, dst) in enumerate(pairs)
    ]
    kept = pltpu.make_async_copy(
        outgoing.at[mine_wide], all_halo.at[mine, mine_wide], local_sem.at[2]
    )
    for copy in own + [kept]:
        copy.start()
    kept.wait()
    for copy in exchange:
        copy.wait_recv()
    block = all_halo.at[mine]
    to_across.append(push(block, block, send_sem.at[2], recv_sem.at[2], mine_wide, across))
    to_core.append(push(block, block, send_sem.at[5], recv_sem.at[5], mine_wide, core))
    onward = []
    for n, dst in enumerate((all_bits, all_meta, all_halo)):
        to_across[n].wait_recv()
        block = dst.at[across]
        onward.append(push(block, block, send_sem.at[6 + n], recv_sem.at[6 + n], mine_wide, core))
    for copy in to_core + onward:
        copy.wait_recv()
    for copy in to_across + to_core + onward + exchange:
        copy.wait_send()
    for copy in own:
        copy.wait()


def build_adjacency(
    dst_count, halo_blocks, meta, bits, adjacency, low_sum, high_sum, lhs, raised_even, raised_odd
):
    replicas = bits.shape[0]
    per_sum = replicas // 2
    own_pairs = dst_count // 2
    halo_pairs = per_sum * halo_blocks // 2
    pair_count = own_pairs + halo_pairs
    groups = bits.shape[1] // BLOCK
    sums = (low_sum, high_sum)

    for target in sums:
        target[...] = jnp.zeros_like(target)
    for r in range(replicas):
        words = bits[r]
        rows = pl.ds(r * words.shape[0], words.shape[0])
        lhs[rows, :LANES] = (words & 255).astype(jnp.float32).astype(jnp.bfloat16)
        lhs[rows, LANES:] = (words >> 8).astype(jnp.float32).astype(jnp.bfloat16)

    row = lax.broadcasted_iota(jnp.int32, (2 * LANES, 2 * LANES), 0)
    col = lax.broadcasted_iota(jnp.int32, (2 * LANES, 2 * LANES), 1)
    bit = col & (BLOCK - 1)
    match = (((row >> 5) & 3) == (bit >> 4)) & ((row >> 7) == ((bit >> 3) & 1))
    factor = (1 << (7 - (bit & 7))).astype(jnp.float32) * (1.0 / 128.0)
    pattern = jnp.where(match, factor, 0.0)
    behind = (row & (GROUP - 1)) - (col >> 7)
    lane_half = lax.broadcasted_iota(jnp.int32, (1, LANES), 1) >> 6

    def expand(n):
        chosen = jnp.where(behind == 2 * n, pattern, 0.0).astype(jnp.bfloat16)
        return jnp.dot(lhs[...], chosen, preferred_element_type=jnp.float32)

    def add_tiles(raised, n):
        for g in range(groups):
            for t in range(2):
                for turn in range(replicas):
                    r = (turn % 2) * per_sum + turn // 2
                    place = g * GROUP + 2 * n + t
                    dst = meta[r, 0, place]
                    src = meta[r, 1, place]
                    column = jnp.where(src < dst_count, src, src + (r % per_sum) * halo_blocks)
                    where = dst * pair_count + (column >> 1)
                    keep = jnp.where(lane_half == (column & 1), 1, 0)
                    first = (r * groups + g) * BLOCK
                    part = raised[first : first + BLOCK, t * LANES : (t + 1) * LANES]
                    sums[r // per_sum][where] += (
                        (part.astype(jnp.int32) & keep).astype(jnp.float32).astype(jnp.bfloat16)
                    )

    raised_even[...] = expand(0)

    def four_tiles(m, carry):
        raised_odd[...] = expand(2 * m + 1)
        add_tiles(raised_even, 2 * m)
        raised_even[...] = expand(2 * m + 2)
        add_tiles(raised_odd, 2 * m + 1)
        return carry

    lax.fori_loop(0, GROUP // 4, four_tiles, 0)

    def place_row(b, carry):
        rows = pl.ds(pl.multiple_of(b * BLOCK, BLOCK), BLOCK)
        for p in range(own_pairs):
            both = low_sum[b * pair_count + p].astype(jnp.float32) + high_sum[
                b * pair_count + p
            ].astype(jnp.float32)
            adjacency[rows, p * LANES : (p + 1) * LANES] = both.astype(jnp.bfloat16)
        for n, target in enumerate(sums):
            for p in range(halo_pairs):
                start = (own_pairs + n * halo_pairs + p) * LANES
                adjacency[rows, start : start + LANES] = target[b * pair_count + own_pairs + p]
        return carry

    lax.fori_loop(0, dst_count, place_row, 0)


def layer(
    peer_count,
    slots,
    reduce_here,
    adjacency_from,
    halo,
    meta,
    grad_own,
    grad_core,
    grad_across,
    grad_diagonal,
    feats,
    w_self,
    w_neigh,
    norm,
    out_feats,
    grad_feats,
    weights,
    weight_grad,
    adjacency,
    table,
    scale,
    agg,
    grad_pre,
    grad_agg,
    halo_grad,
    halo_out,
    came_halo,
    came_weight,
    summed,
    local_sem,
    halo_send,
    halo_recv,
    part_send,
    part_recv,
    full_send,
    full_recv,
    rep_send,
    rep_recv,
    back_send,
    back_recv,
    fetch_sem,
):
    mine_wide = lax.axis_index("wide")
    mine, core, across, diagonal = partners(4)
    barrier = greet(peer_count, mine_wide, mine, core, across)
    replicas = meta.shape[0]
    node_rows, width = feats.shape
    halo_rows = peer_count * slots
    quarter = node_rows // replicas
    share = width // replicas
    rows = 2 * share // peer_count
    per_half = peer_count // 2

    def rows_of(q):
        return pl.ds(pl.multiple_of(q * quarter, quarter), quarter)

    fetches = [
        pltpu.make_async_copy(
            adjacency_from.at[rows_of(q)], adjacency.at[rows_of(q)], fetch_sem.at[n]
        )
        for n, q in enumerate((mine, core, across, diagonal))
    ]
    for copy in fetches:
        copy.start()
    table[:node_rows, :] = feats[...]
    for r in range(replicas):
        for first in range(0, peer_count, 8):
            start = node_rows + r * halo_rows + first * slots
            table[start : start + 8 * slots, :] = unfolded(halo[r, first : first + 8])
    eye = lax.broadcasted_iota(jnp.int32, (LANES, LANES), 0) == lax.broadcasted_iota(
        jnp.int32, (LANES, LANES), 1
    )
    for n in range(node_rows // LANES):
        counts = norm[n : n + 1, :].astype(jnp.float32)
        column = jnp.sum(jnp.where(eye, counts, 0.0), axis=1, keepdims=True)
        scale[n * LANES : (n + 1) * LANES, :] = lax.rsqrt(column)

    parts = ((mine, grad_own), (core, grad_core), (across, grad_across), (diagonal, grad_diagonal))
    for (q, grad_out), fetch in zip(parts, fetches):
        here = rows_of(q)
        fetch.wait()
        sums = jnp.dot(adjacency[here, :], table[...], preferred_element_type=jnp.float32)
        part_scale = scale[here, :]
        part_agg = (sums * part_scale).astype(jnp.bfloat16)
        agg[here, :] = part_agg
        pre = jnp.dot(feats[here, :], w_self[...], preferred_element_type=jnp.float32) + jnp.dot(
            part_agg, w_neigh[...], preferred_element_type=jnp.float32
        )
        sig = jax.nn.sigmoid(pre)
        if grad_out is grad_own:
            out_feats[...] = (pre * sig).astype(jnp.bfloat16)
        back = (grad_out[...].astype(jnp.float32) * sig * (1.0 + pre * (1.0 - sig))).astype(
            jnp.bfloat16
        )
        grad_pre[here, :] = back
        grad_agg[here, :] = (times_transposed(back, w_neigh[...]) * part_scale).astype(
            jnp.bfloat16
        )

    columns = pl.ds(pl.multiple_of(mine * share, share), share)
    weight_grad[:share, :] = transposed_times(feats[:, columns], grad_pre[...]).astype(
        jnp.bfloat16
    )
    weight_grad[share:, :] = transposed_times(agg[:, columns], grad_pre[...]).astype(jnp.bfloat16)
    pl.semaphore_wait(barrier, peer_count + 1)

    def place(owner_wide, owner_rep):
        start = owner_rep * share + lax.rem(owner_wide, per_half) * rows
        return weights.at[owner_wide // per_half, pl.ds(pl.multiple_of(start, rows), rows)]

    part_copies, halo_copies = [], []
    if reduce_here:
        for step in range(1, peer_count):
            peer = lax.rem(mine_wide + step, peer_count)
            piece = weight_grad.at[pl.ds(pl.multiple_of(peer * rows, rows), rows)]
            part_copies.append(
                push(
                    piece, came_weight.at[step], part_send.at[step], part_recv.at[step], peer, mine
                )
            )

    block = min(replicas * halo_rows, 512)
    for first in range(0, replicas * halo_rows, block):
        start = node_rows + first
        halo_grad[first : first + block, :] = transposed_times(
            adjacency[:, start : start + block], grad_agg[...]
        )
    for n in range(peer_count):
        start = pl.multiple_of(mine * halo_rows, 8) + n * slots
        halo_out[n] = folded(halo_grad[pl.ds(pl.multiple_of(start, 8), slots), :])
    for step in range(1, peer_count):
        peer = lax.rem(mine_wide + step, peer_count)
        halo_copies.append(
            push(
                halo_out.at[peer],
                came_halo.at[mine, mine_wide],
                halo_send.at[step],
                halo_recv.at[step],
                peer,
                mine,
            )
        )
    kept = pltpu.make_async_copy(
        halo_out.at[mine_wide], came_halo.at[mine, mine_wide], local_sem.at[0]
    )
    kept.start()
    own_rows = rows_of(mine)
    total_grad = transposed_times(adjacency[:, own_rows], grad_agg[...]) + times_transposed(
        grad_pre[own_rows, :], w_self[...]
    )

    if reduce_here:
        total = weight_grad[pl.ds(pl.multiple_of(mine_wide * rows, rows), rows), :].astype(
            jnp.float32
        )
        for step in range(1, peer_count):
            part_copies[step - 1].wait_recv()
            total = total + came_weight[step].astype(jnp.float32)
        summed[...] = total.astype(jnp.bfloat16)
        spot = place(mine_wide, mine)
        beside = mine_wide + 1 - 2 * lax.rem(mine_wide, 2)
        hops = list(range(1, per_half))
        full_copies = {}
        across_copies, core_copies = {}, {}

        def share_piece(slot, src, dst):
            across_copies[slot] = push(
                src, dst, rep_send.at[0, slot], rep_recv.at[0, slot], mine_wide, across
            )
            core_copies[slot] = push(
                src, dst, rep_send.at[1, slot], rep_recv.at[1, slot], mine_wide, core
            )

        def owner_of(slot):
            base = mine_wide if slot < per_half else beside
            return lax.rem(base + peer_count - 2 * (slot % per_half), peer_count)

        full_copies[per_half] = push(
            summed, spot, full_send.at[per_half], full_recv.at[per_half], beside, mine
        )
        share_piece(0, summed, spot)
        for hop in hops:
            peer = lax.rem(mine_wide + 2 * hop, peer_count)
            full_copies[hop] = push(
                summed, spot, full_send.at[hop], full_recv.at[hop], peer, mine
            )
        own_slice = pltpu.make_async_copy(summed, spot, local_sem.at[1])
        own_slice.start()

    kept.wait()
    for copy in halo_copies:
        copy.wait_recv()
    block = came_halo.at[mine]
    back_across = push(block, block, back_send.at[0], back_recv.at[0], mine_wide, across)
    back_core = push(block, block, back_send.at[1], back_recv.at[1], mine_wide, core)

    if reduce_here:
        order = [per_half] + sorted(hops, key=lambda hop: min(hop, per_half - hop))
        order = order + [per_half + hop for hop in order[1:]]
        for slot in order:
            full_copies[slot].wait_recv()
            spot = place(owner_of(slot), mine)
            if slot < per_half:
                ahead = per_half + slot
                full_copies[ahead] = push(
                    spot, spot, full_send.at[ahead], full_recv.at[ahead], beside, mine
                )
            share_piece(slot, spot, spot)

    back_across.wait_recv()
    block = came_halo.at[across]
    back_onward = push(block, block, back_send.at[2], back_recv.at[2], mine_wide, core)
    back_core.wait_recv()
    back_onward.wait_recv()
    for r in range(replicas):
        for first in range(0, peer_count, 8):
            picks = as_column(meta[r, 8 + first : 16 + first, :slots]) - mine * quarter
            chosen = picks == lax.broadcasted_iota(jnp.int32, (8 * slots, quarter), 1)
            total_grad = total_grad + transposed_times(
                jnp.where(chosen, 1.0, 0.0).astype(jnp.bfloat16),
                unfolded(came_halo[r, first : first + 8]),
            )
    grad_feats[...] = total_grad.astype(jnp.bfloat16)

    if reduce_here:
        onward = []
        for slot in [0] + order:
            across_copies[slot].wait_recv()
            spot = place(owner_of(slot), across)
            onward.append(
                push(spot, spot, rep_send.at[2, slot], rep_recv.at[2, slot], mine_wide, core)
            )
        sent = list(full_copies.values()) + list(across_copies.values())
        sent = sent + list(core_copies.values()) + onward
        for copy in list(core_copies.values()) + onward:
            copy.wait_recv()
        for copy in part_copies + sent:
            copy.wait_send()
        own_slice.wait()
    for copy in halo_copies + [back_across, back_core, back_onward]:
        copy.wait_send()


def deliver(out_feats, grad_feats, weights, out_to, grad_to, self_to, neigh_to, sems):
    pairs = (
        (out_feats, out_to),
        (grad_feats, grad_to),
        (weights.at[0], self_to),
        (weights.at[1], neigh_to),
    )
    copies = [pltpu.make_async_copy(src, dst, sems.at[n]) for n, (src, dst) in enumerate(pairs)]
    for copy in copies:
        copy.start()
    for copy in copies:
        copy.wait()


def on_device(
    node_feats, w_self, w_neigh, send_rows, tile_dst, tile_src, tile_bits, norm_count, grad_out
):
    node_rows, width = node_feats.shape
    peer_count = lax.axis_size("wide")
    replicas = lax.axis_size("rep")
    slots = send_rows.shape[2]
    tile_total = tile_dst.shape[2]
    quarter = node_rows // replicas
    halo_rows = peer_count * slots
    halo_blocks = halo_rows // BLOCK
    words = tile_bits.reshape(-1, LANES)
    any_spec = pl.BlockSpec(memory_space=pl.ANY)
    vmem_spec = pl.BlockSpec(memory_space=pltpu.VMEM)
    smem_spec = pl.BlockSpec(memory_space=pltpu.SMEM)

    def shaped(dims, held):
        return jax.ShapeDtypeStruct(dims, held)

    def dma(*dims):
        return pltpu.SemaphoreType.DMA(dims)

    by_core = [(n, n + 1 - 2 * (n % 2)) for n in range(replicas)]
    by_chip = [(n, (n + 2) % replicas) for n in range(replicas)]
    grad_across = lax.ppermute(grad_out, "rep", by_chip)
    grad_core = lax.ppermute(grad_out, "rep", by_core)
    grad_diagonal = lax.ppermute(grad_across, "rep", by_core)

    halo_shape = (replicas, peer_count, 2 * slots, width // 2)
    meta_shape = (8 + peer_count, tile_total)
    with jax.named_scope("spread_inputs"):
        all_bits, all_meta, all_halo = pl.pallas_call(
            functools.partial(spread_inputs, peer_count, slots),
            out_shape=(
                shaped((replicas,) + words.shape, jnp.int32),
                shaped((replicas,) + meta_shape, jnp.int32),
                shaped(halo_shape, jnp.bfloat16),
            ),
            in_specs=[vmem_spec] * 5,
            out_specs=(vmem_spec,) * 3,
            scratch_shapes=[
                pltpu.VMEM(words.shape, jnp.int32),
                pltpu.VMEM(meta_shape, jnp.int32),
                pltpu.VMEM(halo_shape[1:], jnp.bfloat16),
                dma(3),
                dma(9),
                dma(9),
                dma(peer_count),
                dma(peer_count),
            ],
            compiler_params=pltpu.CompilerParams(
                collective_id=0, has_side_effects=True, vmem_limit_bytes=VMEM_BYTES
            ),
        )(words, tile_dst[0], tile_src[0], send_rows[0], node_feats)

    columns = node_rows + replicas * halo_rows
    dst_count = node_rows // BLOCK
    sum_shape = (dst_count * (dst_count + replicas // 2 * halo_blocks) // 2, BLOCK, LANES)
    with jax.named_scope("build_adjacency"):
        adjacency = pl.pallas_call(
            functools.partial(build_adjacency, dst_count, halo_blocks),
            out_shape=shaped((node_rows, columns), jnp.bfloat16),
            in_specs=[smem_spec, vmem_spec],
            out_specs=vmem_spec,
            scratch_shapes=[
                pltpu.VMEM(sum_shape, jnp.bfloat16),
                pltpu.VMEM(sum_shape, jnp.bfloat16),
                pltpu.VMEM((replicas * words.shape[0], 2 * LANES), jnp.bfloat16),
                pltpu.VMEM((replicas * words.shape[0], 2 * LANES), jnp.float32),
                pltpu.VMEM((replicas * words.shape[0], 2 * LANES), jnp.float32),
            ],
            compiler_params=pltpu.CompilerParams(vmem_limit_bytes=VMEM_BYTES),
            cost_estimate=pl.CostEstimate(
                flops=8 * 10**9, bytes_accessed=4 * 10**6, transcendentals=0
            ),
        )(all_meta, all_bits)

    rows = 2 * width // replicas // peer_count
    reduce_here = rows % 16 == 0
    piece = (rows if reduce_here else 16, width)
    with jax.named_scope("layer"):
        out_feats, grad_feats, weights, weight_grad = pl.pallas_call(
            functools.partial(layer, peer_count, slots, reduce_here),
            out_shape=(
                shaped((quarter, width), jnp.bfloat16),
                shaped((quarter, width), jnp.bfloat16),
                shaped((2, width, width), jnp.bfloat16),
                shaped((2 * width // replicas, width), jnp.bfloat16),
            ),
            in_specs=[any_spec] + [vmem_spec] * 10,
            out_specs=(vmem_spec,) * 4,
            scratch_shapes=[
                pltpu.VMEM((node_rows, columns), jnp.bfloat16),
                pltpu.VMEM((columns, width), jnp.bfloat16),
                pltpu.VMEM((node_rows, 1), jnp.float32),
                pltpu.VMEM((node_rows, width), jnp.bfloat16),
                pltpu.VMEM((node_rows, width), jnp.bfloat16),
                pltpu.VMEM((node_rows, width), jnp.bfloat16),
                pltpu.VMEM((replicas * halo_rows, width), jnp.float32),
                pltpu.VMEM(halo_shape[1:], jnp.bfloat16),
                pltpu.VMEM(halo_shape, jnp.bfloat16),
                pltpu.VMEM((peer_count,) + piece, jnp.bfloat16),
                pltpu.VMEM(piece, jnp.bfloat16),
                dma(2),
            ]
            + [dma(peer_count)] * 6
            + [dma(3, peer_count)] * 2
            + [dma(3)] * 2
            + [dma(replicas)],
            compiler_params=pltpu.CompilerParams(
                collective_id=1, has_side_effects=True, vmem_limit_bytes=VMEM_BYTES
            ),
        )(
            adjacency,
            all_halo,
            all_meta,
            grad_out,
            grad_core,
            grad_across,
            grad_diagonal,
            node_feats,
            w_self,
            w_neigh,
            norm_count.reshape(-1, LANES),
        )
    if reduce_here:
        with jax.named_scope("deliver"):
            return pl.pallas_call(
                deliver,
                out_shape=(
                    shaped((quarter, width), jnp.bfloat16),
                    shaped((quarter, width), jnp.bfloat16),
                    shaped((width, width), jnp.bfloat16),
                    shaped((width, width), jnp.bfloat16),
                ),
                in_specs=[vmem_spec] * 3,
                out_specs=(any_spec,) * 4,
                scratch_shapes=[dma(4)],
            )(out_feats, grad_feats, weights)
    total = lax.psum(weight_grad.astype(jnp.float32), "wide").astype(jnp.bfloat16)
    whole = lax.all_gather(total, "rep", axis=0, tiled=False)
    share = width // replicas
    return (
        out_feats,
        grad_feats,
        whole[:, :share].reshape(width, width),
        whole[:, share:].reshape(width, width),
    )


def solution(mesh):
    in_specs = (
        P("wide", None),
        P(),
        P(),
        P("wide", None, "rep"),
        P("wide", "rep", None),
        P("wide", "rep", None),
        P("wide", "rep", None),
        P("wide"),
        P(("wide", "rep"), None),
    )
    out_specs = (P(("wide", "rep"), None), P(("wide", "rep"), None), P(), P())
    return jax.shard_map(
        on_device, mesh=mesh, in_specs=in_specs, out_specs=out_specs, check_vma=False
    )
```

```python
import functools

import jax
import jax.numpy as jnp
from jax import lax
from jax.experimental import pallas as pl
from jax.experimental.pallas import tpu as pltpu
from jax.sharding import PartitionSpec as P

BLOCK = 64
GROUP = 32
LANES = 128
MESH = pl.DeviceIdType.MESH
VMEM_BYTES = 56 * 1024 * 1024


def partners(replicas):
    mine = lax.axis_index("rep")
    core = mine + 1 - 2 * lax.rem(mine, 2)
    across = lax.rem(mine + 2, replicas)
    diagonal = lax.rem(core + 2, replicas)
    return mine, core, across, diagonal


def times_transposed(left, right):
    return lax.dot_general(
        left, right, (((1,), (1,)), ((), ())), preferred_element_type=jnp.float32
    )


def transposed_times(left, right):
    return lax.dot_general(
        left, right, (((0,), (0,)), ((), ())), preferred_element_type=jnp.float32
    )


def as_column(picks):
    count, slots = picks.shape
    same = lax.broadcasted_iota(jnp.int32, (count, slots, slots), 1) == lax.broadcasted_iota(
        jnp.int32, (count, slots, slots), 2
    )
    wide = jnp.broadcast_to(picks.astype(jnp.float32)[:, None, :], (count, slots, slots))
    column = jnp.sum(jnp.where(same, wide, 0.0), axis=2, keepdims=True)
    return column.reshape(count * slots, 1).astype(jnp.int32)


def folded(part):
    half = part.shape[1] // 2
    return jnp.concatenate([part[:, :half], part[:, half:]], axis=0).astype(jnp.bfloat16)


def unfolded(parts):
    count, rows, half = parts.shape
    wide = parts.astype(jnp.float32)
    joined = jnp.concatenate([wide[:, : rows // 2, :], wide[:, rows // 2 :, :]], axis=2)
    return joined.reshape(count * rows // 2, 2 * half).astype(jnp.bfloat16)


def sort_words(words, sorted_words):
    rows = lax.broadcasted_iota(jnp.int32, (LANES, LANES), 0)
    lanes = lax.broadcasted_iota(jnp.int32, (LANES, LANES), 1)
    wanted = (rows // GROUP) == lanes % 4
    pick_row = lax.broadcasted_iota(jnp.int32, (GROUP, 2 * LANES), 0)
    pick_lane = lax.broadcasted_iota(jnp.int32, (GROUP, 2 * LANES), 1) % LANES
    pick = jnp.where(pick_row == pick_lane // 4, 1.0, 0.0).astype(jnp.bfloat16)
    for group in range(words.shape[0] // BLOCK):
        for h in range(2):
            part = words[pl.ds(group * BLOCK + h, GROUP, stride=2), :]
            low = (part & 255).astype(jnp.float32)
            high = (part - (part & 255)).astype(jnp.float32)
            both = jnp.concatenate(
                [
                    jnp.where(wanted, jnp.concatenate([half] * 4, axis=0), 0.0)
                    for half in (low, high)
                ],
                axis=1,
            ).astype(jnp.bfloat16)
            start = group * BLOCK + h * GROUP
            sorted_words[start : start + GROUP, :] = times_transposed(pick, both).astype(jnp.int32)


def greet(peer_count, mine_wide, mine, core, across):
    barrier = pltpu.get_barrier_semaphore()
    for step in range(1, peer_count):
        peer = lax.rem(mine_wide + step, peer_count)
        pl.semaphore_signal(barrier, inc=1, device_id=(peer, mine), device_id_type=MESH)
    for other in (core, across):
        pl.semaphore_signal(barrier, inc=1, device_id=(mine_wide, other), device_id_type=MESH)
    return barrier


def push(src, dst, send, recv, wide_to, rep_to):
    copy = pltpu.make_async_remote_copy(
        src_ref=src,
        dst_ref=dst,
        send_sem=send,
        recv_sem=recv,
        device_id=(wide_to, rep_to),
        device_id_type=MESH,
    )
    copy.start()
    return copy


def spread_inputs(
    peer_count,
    slots,
    words,
    tile_dst,
    tile_src,
    send_rows,
    feats,
    all_bits,
    all_meta,
    all_halo,
    bits,
    meta,
    outgoing,
    local_sem,
    send_sem,
    recv_sem,
    halo_send,
    halo_recv,
):
    mine_wide = lax.axis_index("wide")
    mine, core, across, diagonal = partners(4)
    barrier = greet(peer_count, mine_wide, mine, core, across)
    meta[...] = jnp.zeros_like(meta)
    meta[0:1, :] = tile_dst[...]
    meta[1:2, :] = tile_src[...]
    meta[8:, :slots] = send_rows[...]
    node_rows = feats.shape[0]
    for first in range(0, peer_count, 8):
        picks = as_column(send_rows[first : first + 8, :])
        chosen = picks == lax.broadcasted_iota(jnp.int32, (8 * slots, node_rows), 1)
        rows = jnp.dot(
            jnp.where(chosen, 1.0, 0.0).astype(jnp.bfloat16),
            feats[...],
            preferred_element_type=jnp.float32,
        )
        for n in range(8):
            outgoing[first + n] = folded(rows[n * slots : (n + 1) * slots])
    sort_words(words, bits)
    pl.semaphore_wait(barrier, peer_count + 1)

    exchange = []
    for step in range(1, peer_count):
        peer = lax.rem(mine_wide + step, peer_count)
        exchange.append(
            push(
                outgoing.at[peer],
                all_halo.at[mine, mine_wide],
                halo_send.at[step],
                halo_recv.at[step],
                peer,
                mine,
            )
        )
    pairs = ((bits, all_bits), (meta, all_meta))
    to_across = [
        push(src, dst.at[mine], send_sem.at[n], recv_sem.at[n], mine_wide, across)
        for n, (src, dst) in enumerate(pairs)
    ]
    to_core = [
        push(src, dst.at[mine], send_sem.at[3 + n], recv_sem.at[3 + n], mine_wide, core)
        for n, (src, dst) in enumerate(pairs)
    ]
    own = [
        pltpu.make_async_copy(src, dst.at[mine], local_sem.at[n])
        for n, (src, dst) in enumerate(pairs)
    ]
    kept = pltpu.make_async_copy(
        outgoing.at[mine_wide], all_halo.at[mine, mine_wide], local_sem.at[2]
    )
    for copy in own + [kept]:
        copy.start()
    kept.wait()
    for copy in exchange:
        copy.wait_recv()
    block = all_halo.at[mine]
    to_across.append(push(block, block, send_sem.at[2], recv_sem.at[2], mine_wide, across))
    to_core.append(push(block, block, send_sem.at[5], recv_sem.at[5], mine_wide, core))
    onward = []
    for n, dst in enumerate((all_bits, all_meta, all_halo)):
        to_across[n].wait_recv()
        block = dst.at[across]
        onward.append(push(block, block, send_sem.at[6 + n], recv_sem.at[6 + n], mine_wide, core))
    for copy in to_core + onward:
        copy.wait_recv()
    for copy in to_across + to_core + onward + exchange:
        copy.wait_send()
    for copy in own:
        copy.wait()


def build_adjacency(
    dst_count, halo_blocks, meta, bits, adjacency, low_sum, high_sum, lhs, raised_even, raised_odd
):
    replicas = bits.shape[0]
    per_sum = replicas // 2
    own_pairs = dst_count // 2
    halo_pairs = per_sum * halo_blocks // 2
    pair_count = own_pairs + halo_pairs
    groups = bits.shape[1] // BLOCK
    sums = (low_sum, high_sum)

    for target in sums:
        target[...] = jnp.zeros_like(target)
    for r in range(replicas):
        words = bits[r]
        rows = pl.ds(r * words.shape[0], words.shape[0])
        lhs[rows, :LANES] = (words & 255).astype(jnp.float32).astype(jnp.bfloat16)
        lhs[rows, LANES:] = (words >> 8).astype(jnp.float32).astype(jnp.bfloat16)

    row = lax.broadcasted_iota(jnp.int32, (2 * LANES, 2 * LANES), 0)
    col = lax.broadcasted_iota(jnp.int32, (2 * LANES, 2 * LANES), 1)
    bit = col & (BLOCK - 1)
    match = (((row >> 5) & 3) == (bit >> 4)) & ((row >> 7) == ((bit >> 3) & 1))
    factor = (1 << (7 - (bit & 7))).astype(jnp.float32) * (1.0 / 128.0)
    pattern = jnp.where(match, factor, 0.0)
    behind = (row & (GROUP - 1)) - (col >> 7)
    lane_half = lax.broadcasted_iota(jnp.int32, (1, LANES), 1) >> 6

    def expand(n):
        chosen = jnp.where(behind == 2 * n, pattern, 0.0).astype(jnp.bfloat16)
        return jnp.dot(lhs[...], chosen, preferred_element_type=jnp.float32)

    def add_tiles(raised, n):
        for g in range(groups):
            for t in range(2):
                for turn in range(replicas):
                    r = (turn % 2) * per_sum + turn // 2
                    place = g * GROUP + 2 * n + t
                    dst = meta[r, 0, place]
                    src = meta[r, 1, place]
                    column = jnp.where(src < dst_count, src, src + (r % per_sum) * halo_blocks)
                    where = dst * pair_count + (column >> 1)
                    keep = jnp.where(lane_half == (column & 1), 1, 0)
                    first = (r * groups + g) * BLOCK
                    part = raised[first : first + BLOCK, t * LANES : (t + 1) * LANES]
                    sums[r // per_sum][where] += (
                        (part.astype(jnp.int32) & keep).astype(jnp.float32).astype(jnp.bfloat16)
                    )

    raised_even[...] = expand(0)

    def four_tiles(m, carry):
        raised_odd[...] = expand(2 * m + 1)
        add_tiles(raised_even, 2 * m)
        raised_even[...] = expand(2 * m + 2)
        add_tiles(raised_odd, 2 * m + 1)
        return carry

    lax.fori_loop(0, GROUP // 4, four_tiles, 0)

    def place_row(b, carry):
        rows = pl.ds(pl.multiple_of(b * BLOCK, BLOCK), BLOCK)
        for p in range(own_pairs):
            both = low_sum[b * pair_count + p].astype(jnp.float32) + high_sum[
                b * pair_count + p
            ].astype(jnp.float32)
            adjacency[rows, p * LANES : (p + 1) * LANES] = both.astype(jnp.bfloat16)
        for n, target in enumerate(sums):
            for p in range(halo_pairs):
                start = (own_pairs + n * halo_pairs + p) * LANES
                adjacency[rows, start : start + LANES] = target[b * pair_count + own_pairs + p]
        return carry

    lax.fori_loop(0, dst_count, place_row, 0)


def layer(
    peer_count,
    slots,
    reduce_here,
    adjacency_from,
    halo,
    meta,
    grad_own,
    grad_across,
    feats,
    w_self,
    w_neigh,
    norm,
    out_feats,
    grad_feats,
    weights,
    weight_grad,
    grad_core,
    grad_diagonal,
    adjacency,
    table,
    scale,
    agg,
    grad_pre,
    grad_agg,
    halo_grad,
    halo_out,
    came_halo,
    came_weight,
    summed,
    local_sem,
    halo_send,
    halo_recv,
    part_send,
    part_recv,
    full_send,
    full_recv,
    rep_send,
    rep_recv,
    back_send,
    back_recv,
    fetch_sem,
    out_send,
    out_recv,
):
    mine_wide = lax.axis_index("wide")
    mine, core, across, diagonal = partners(4)
    barrier = greet(peer_count, mine_wide, mine, core, across)
    replicas = meta.shape[0]
    node_rows, width = feats.shape
    halo_rows = peer_count * slots
    quarter = node_rows // replicas
    share = width // replicas
    rows = 2 * share // peer_count
    per_half = peer_count // 2

    def rows_of(q):
        return pl.ds(pl.multiple_of(q * quarter, quarter), quarter)

    fetches = [
        pltpu.make_async_copy(
            adjacency_from.at[rows_of(q)], adjacency.at[rows_of(q)], fetch_sem.at[n]
        )
        for n, q in enumerate((mine, across, core, diagonal))
    ]
    for copy in fetches:
        copy.start()
    table[:node_rows, :] = feats[...]
    for r in range(replicas):
        for first in range(0, peer_count, 8):
            start = node_rows + r * halo_rows + first * slots
            table[start : start + 8 * slots, :] = unfolded(halo[r, first : first + 8])
    eye = lax.broadcasted_iota(jnp.int32, (LANES, LANES), 0) == lax.broadcasted_iota(
        jnp.int32, (LANES, LANES), 1
    )
    for n in range(node_rows // LANES):
        counts = norm[n : n + 1, :].astype(jnp.float32)
        column = jnp.sum(jnp.where(eye, counts, 0.0), axis=1, keepdims=True)
        scale[n * LANES : (n + 1) * LANES, :] = lax.rsqrt(column)

    pl.semaphore_wait(barrier, peer_count + 1)
    to_core = push(grad_own, grad_core, out_send.at[0], out_recv.at[0], mine_wide, core)
    onto_core = push(grad_across, grad_diagonal, out_send.at[1], out_recv.at[1], mine_wide, core)
    parts = (
        (mine, grad_own, None),
        (across, grad_across, None),
        (core, grad_core, to_core),
        (diagonal, grad_diagonal, onto_core),
    )
    for (q, grad_out, arrival), fetch in zip(parts, fetches):
        here = rows_of(q)
        fetch.wait()
        if arrival is not None:
            arrival.wait()
        sums = jnp.dot(adjacency[here, :], table[...], preferred_element_type=jnp.float32)
        part_scale = scale[here, :]
        part_agg = (sums * part_scale).astype(jnp.bfloat16)
        agg[here, :] = part_agg
        pre = jnp.dot(feats[here, :], w_self[...], preferred_element_type=jnp.float32) + jnp.dot(
            part_agg, w_neigh[...], preferred_element_type=jnp.float32
        )
        sig = jax.nn.sigmoid(pre)
        if grad_out is grad_own:
            out_feats[...] = (pre * sig).astype(jnp.bfloat16)
        back = (grad_out[...].astype(jnp.float32) * sig * (1.0 + pre * (1.0 - sig))).astype(
            jnp.bfloat16
        )
        grad_pre[here, :] = back
        grad_agg[here, :] = (times_transposed(back, w_neigh[...]) * part_scale).astype(
            jnp.bfloat16
        )

    columns = pl.ds(pl.multiple_of(mine * share, share), share)
    weight_grad[:share, :] = transposed_times(feats[:, columns], grad_pre[...]).astype(
        jnp.bfloat16
    )
    weight_grad[share:, :] = transposed_times(agg[:, columns], grad_pre[...]).astype(jnp.bfloat16)

    def place(owner_wide, owner_rep):
        start = owner_rep * share + owner_wide // 2 * rows
        return weights.at[lax.rem(owner_wide, 2), pl.ds(pl.multiple_of(start, rows), rows)]

    def half_of(parity, owner_rep):
        return weights.at[parity, pl.ds(pl.multiple_of(owner_rep * share, share), share)]

    def slice_of(owner_wide):
        start = (lax.rem(owner_wide, 2) * per_half + owner_wide // 2) * rows
        return pl.ds(pl.multiple_of(start, rows), rows)

    part_copies, halo_copies = [], []
    if reduce_here:
        for step in range(1, peer_count):
            peer = lax.rem(mine_wide + step, peer_count)
            piece = weight_grad.at[slice_of(peer)]
            part_copies.append(
                push(
                    piece, came_weight.at[step], part_send.at[step], part_recv.at[step], peer, mine
                )
            )

    block = min(replicas * halo_rows, 512)
    for first in range(0, replicas * halo_rows, block):
        start = node_rows + first
        halo_grad[first : first + block, :] = transposed_times(
            adjacency[:, start : start + block], grad_agg[...]
        )
    for n in range(peer_count):
        start = pl.multiple_of(mine * halo_rows, 8) + n * slots
        halo_out[n] = folded(halo_grad[pl.ds(pl.multiple_of(start, 8), slots), :])
    for step in range(1, peer_count):
        peer = lax.rem(mine_wide + step, peer_count)
        halo_copies.append(
            push(
                halo_out.at[peer],
                came_halo.at[mine, mine_wide],
                halo_send.at[step],
                halo_recv.at[step],
                peer,
                mine,
            )
        )
    kept = pltpu.make_async_copy(
        halo_out.at[mine_wide], came_halo.at[mine, mine_wide], local_sem.at[0]
    )
    kept.start()
    own_rows = rows_of(mine)
    total_grad = transposed_times(adjacency[:, own_rows], grad_agg[...]) + times_transposed(
        grad_pre[own_rows, :], w_self[...]
    )

    if reduce_here:
        total = weight_grad[slice_of(mine_wide), :].astype(jnp.float32)
        for step in range(1, peer_count):
            part_copies[step - 1].wait_recv()
            total = total + came_weight[step].astype(jnp.float32)
        summed[...] = total.astype(jnp.bfloat16)
        spot = place(mine_wide, mine)
        parity = lax.rem(mine_wide, 2)
        beside = mine_wide + 1 - 2 * parity
        own_slice = pltpu.make_async_copy(summed, spot, local_sem.at[1])
        own_slice.start()
        full_copies = []
        for hop in range(1, per_half):
            peer = lax.rem(mine_wide + 2 * hop, peer_count)
            full_copies.append(
                push(summed, spot, full_send.at[hop], full_recv.at[hop], peer, mine)
            )

    kept.wait()
    for copy in halo_copies:
        copy.wait_recv()
    block = came_halo.at[mine]
    back_across = push(block, block, back_send.at[0], back_recv.at[0], mine_wide, across)
    back_core = push(block, block, back_send.at[1], back_recv.at[1], mine_wide, core)

    if reduce_here:
        across_copies, core_copies = [], []

        def share_half(n, block):
            across_copies.append(
                push(block, block, rep_send.at[0, n], rep_recv.at[0, n], mine_wide, across)
            )
            core_copies.append(
                push(block, block, rep_send.at[1, n], rep_recv.at[1, n], mine_wide, core)
            )

        own_slice.wait()
        for copy in full_copies:
            copy.wait_recv()
        block = half_of(parity, mine)
        swap = push(block, block, full_send.at[0], full_recv.at[0], beside, mine)
        share_half(0, block)
        swap.wait_recv()
        share_half(1, half_of(1 - parity, mine))

    back_across.wait_recv()
    block = came_halo.at[across]
    back_onward = push(block, block, back_send.at[2], back_recv.at[2], mine_wide, core)
    back_core.wait_recv()
    back_onward.wait_recv()
    for r in range(replicas):
        for first in range(0, peer_count, 8):
            picks = as_column(meta[r, 8 + first : 16 + first, :slots]) - mine * quarter
            chosen = picks == lax.broadcasted_iota(jnp.int32, (8 * slots, quarter), 1)
            total_grad = total_grad + transposed_times(
                jnp.where(chosen, 1.0, 0.0).astype(jnp.bfloat16),
                unfolded(came_halo[r, first : first + 8]),
            )
    grad_feats[...] = total_grad.astype(jnp.bfloat16)

    if reduce_here:
        onward = []
        for n, block in enumerate((half_of(parity, across), half_of(1 - parity, across))):
            across_copies[n].wait_recv()
            onward.append(
                push(block, block, rep_send.at[2, n], rep_recv.at[2, n], mine_wide, core)
            )
        for copy in core_copies + onward:
            copy.wait_recv()
        for copy in part_copies + full_copies + [swap] + across_copies + core_copies + onward:
            copy.wait_send()
    for copy in halo_copies + [back_across, back_core, back_onward]:
        copy.wait_send()


def deliver(out_feats, grad_feats, weights, out_to, grad_to, self_to, neigh_to, sems):
    pairs = (
        (out_feats, out_to),
        (grad_feats, grad_to),
        (weights.at[0], self_to),
        (weights.at[1], neigh_to),
    )
    copies = [pltpu.make_async_copy(src, dst, sems.at[n]) for n, (src, dst) in enumerate(pairs)]
    for copy in copies:
        copy.start()
    for copy in copies:
        copy.wait()


def on_device(
    node_feats, w_self, w_neigh, send_rows, tile_dst, tile_src, tile_bits, norm_count, grad_out
):
    node_rows, width = node_feats.shape
    peer_count = lax.axis_size("wide")
    replicas = lax.axis_size("rep")
    slots = send_rows.shape[2]
    tile_total = tile_dst.shape[2]
    quarter = node_rows // replicas
    halo_rows = peer_count * slots
    halo_blocks = halo_rows // BLOCK
    words = tile_bits.reshape(-1, LANES)
    any_spec = pl.BlockSpec(memory_space=pl.ANY)
    vmem_spec = pl.BlockSpec(memory_space=pltpu.VMEM)
    smem_spec = pl.BlockSpec(memory_space=pltpu.SMEM)

    def shaped(dims, held):
        return jax.ShapeDtypeStruct(dims, held)

    def dma(*dims):
        return pltpu.SemaphoreType.DMA(dims)

    halo_shape = (replicas, peer_count, 2 * slots, width // 2)
    meta_shape = (8 + peer_count, tile_total)
    with jax.named_scope("spread_inputs"):
        all_bits, all_meta, all_halo = pl.pallas_call(
            functools.partial(spread_inputs, peer_count, slots),
            out_shape=(
                shaped((replicas,) + words.shape, jnp.int32),
                shaped((replicas,) + meta_shape, jnp.int32),
                shaped(halo_shape, jnp.bfloat16),
            ),
            in_specs=[vmem_spec] * 5,
            out_specs=(vmem_spec,) * 3,
            scratch_shapes=[
                pltpu.VMEM(words.shape, jnp.int32),
                pltpu.VMEM(meta_shape, jnp.int32),
                pltpu.VMEM(halo_shape[1:], jnp.bfloat16),
                dma(3),
                dma(9),
                dma(9),
                dma(peer_count),
                dma(peer_count),
            ],
            compiler_params=pltpu.CompilerParams(
                collective_id=0, has_side_effects=True, vmem_limit_bytes=VMEM_BYTES
            ),
        )(words, tile_dst[0], tile_src[0], send_rows[0], node_feats)

    grad_out, all_bits = lax.optimization_barrier((grad_out, all_bits))
    by_chip = [(n, (n + 2) % replicas) for n in range(replicas)]
    grad_across = lax.ppermute(grad_out, "rep", by_chip)

    columns = node_rows + replicas * halo_rows
    dst_count = node_rows // BLOCK
    sum_shape = (dst_count * (dst_count + replicas // 2 * halo_blocks) // 2, BLOCK, LANES)
    with jax.named_scope("build_adjacency"):
        adjacency = pl.pallas_call(
            functools.partial(build_adjacency, dst_count, halo_blocks),
            out_shape=shaped((node_rows, columns), jnp.bfloat16),
            in_specs=[smem_spec, vmem_spec],
            out_specs=vmem_spec,
            scratch_shapes=[
                pltpu.VMEM(sum_shape, jnp.bfloat16),
                pltpu.VMEM(sum_shape, jnp.bfloat16),
                pltpu.VMEM((replicas * words.shape[0], 2 * LANES), jnp.bfloat16),
                pltpu.VMEM((replicas * words.shape[0], 2 * LANES), jnp.float32),
                pltpu.VMEM((replicas * words.shape[0], 2 * LANES), jnp.float32),
            ],
            compiler_params=pltpu.CompilerParams(vmem_limit_bytes=VMEM_BYTES),
            cost_estimate=pl.CostEstimate(
                flops=8 * 10**9, bytes_accessed=4 * 10**6, transcendentals=0
            ),
        )(all_meta, all_bits)

    rows = 2 * width // replicas // peer_count
    reduce_here = rows % 16 == 0
    piece = (rows if reduce_here else 16, width)
    with jax.named_scope("layer"):
        out_feats, grad_feats, weights, weight_grad = pl.pallas_call(
            functools.partial(layer, peer_count, slots, reduce_here),
            out_shape=(
                shaped((quarter, width), jnp.bfloat16),
                shaped((quarter, width), jnp.bfloat16),
                shaped((2, width, width), jnp.bfloat16),
                shaped((2 * width // replicas, width), jnp.bfloat16),
            ),
            in_specs=[any_spec] + [vmem_spec] * 8,
            out_specs=(vmem_spec,) * 4,
            scratch_shapes=[
                pltpu.VMEM((quarter, width), jnp.bfloat16),
                pltpu.VMEM((quarter, width), jnp.bfloat16),
                pltpu.VMEM((node_rows, columns), jnp.bfloat16),
                pltpu.VMEM((columns, width), jnp.bfloat16),
                pltpu.VMEM((node_rows, 1), jnp.float32),
                pltpu.VMEM((node_rows, width), jnp.bfloat16),
                pltpu.VMEM((node_rows, width), jnp.bfloat16),
                pltpu.VMEM((node_rows, width), jnp.bfloat16),
                pltpu.VMEM((replicas * halo_rows, width), jnp.float32),
                pltpu.VMEM(halo_shape[1:], jnp.bfloat16),
                pltpu.VMEM(halo_shape, jnp.bfloat16),
                pltpu.VMEM((peer_count,) + piece, jnp.bfloat16),
                pltpu.VMEM(piece, jnp.bfloat16),
                dma(2),
            ]
            + [dma(peer_count)] * 6
            + [dma(3, peer_count)] * 2
            + [dma(3)] * 2
            + [dma(replicas)]
            + [dma(2)] * 2,
            compiler_params=pltpu.CompilerParams(
                collective_id=1, has_side_effects=True, vmem_limit_bytes=VMEM_BYTES
            ),
        )(
            adjacency,
            all_halo,
            all_meta,
            grad_out,
            grad_across,
            node_feats,
            w_self,
            w_neigh,
            norm_count.reshape(-1, LANES),
        )
    if reduce_here:
        with jax.named_scope("deliver"):
            return pl.pallas_call(
                deliver,
                out_shape=(
                    shaped((quarter, width), jnp.bfloat16),
                    shaped((quarter, width), jnp.bfloat16),
                    shaped((width, width), jnp.bfloat16),
                    shaped((width, width), jnp.bfloat16),
                ),
                in_specs=[vmem_spec] * 3,
                out_specs=(any_spec,) * 4,
                scratch_shapes=[dma(4)],
            )(out_feats, grad_feats, weights)
    total = lax.psum(weight_grad.astype(jnp.float32), "wide").astype(jnp.bfloat16)
    whole = lax.all_gather(total, "rep", axis=0, tiled=False)
    share = width // replicas
    return (
        out_feats,
        grad_feats,
        whole[:, :share].reshape(width, width),
        whole[:, share:].reshape(width, width),
    )


def solution(mesh):
    in_specs = (
        P("wide", None),
        P(),
        P(),
        P("wide", None, "rep"),
        P("wide", "rep", None),
        P("wide", "rep", None),
        P("wide", "rep", None),
        P("wide"),
        P(("wide", "rep"), None),
    )
    out_specs = (P(("wide", "rep"), None), P(("wide", "rep"), None), P(), P())
    return jax.shard_map(
        on_device, mesh=mesh, in_specs=in_specs, out_specs=out_specs, check_vma=False
    )
```

```python
import functools

import jax
import jax.numpy as jnp
from jax import lax
from jax.experimental import pallas as pl
from jax.experimental.pallas import tpu as pltpu
from jax.sharding import PartitionSpec as P

BLOCK = 64
GROUP = 32
LANES = 128
MESH = pl.DeviceIdType.MESH
VMEM_BYTES = 56 * 1024 * 1024


def partners(replicas):
    mine = lax.axis_index("rep")
    core = mine + 1 - 2 * lax.rem(mine, 2)
    across = lax.rem(mine + 2, replicas)
    diagonal = lax.rem(core + 2, replicas)
    return mine, core, across, diagonal


def times_transposed(left, right):
    return lax.dot_general(
        left, right, (((1,), (1,)), ((), ())), preferred_element_type=jnp.float32
    )


def transposed_times(left, right):
    return lax.dot_general(
        left, right, (((0,), (0,)), ((), ())), preferred_element_type=jnp.float32
    )


def as_column(picks):
    count, slots = picks.shape
    same = lax.broadcasted_iota(jnp.int32, (count, slots, slots), 1) == lax.broadcasted_iota(
        jnp.int32, (count, slots, slots), 2
    )
    wide = jnp.broadcast_to(picks.astype(jnp.float32)[:, None, :], (count, slots, slots))
    column = jnp.sum(jnp.where(same, wide, 0.0), axis=2, keepdims=True)
    return column.reshape(count * slots, 1).astype(jnp.int32)


def folded(part):
    half = part.shape[1] // 2
    return jnp.concatenate([part[:, :half], part[:, half:]], axis=0).astype(jnp.bfloat16)


def unfolded(parts):
    count, rows, half = parts.shape
    wide = parts.astype(jnp.float32)
    joined = jnp.concatenate([wide[:, : rows // 2, :], wide[:, rows // 2 :, :]], axis=2)
    return joined.reshape(count * rows // 2, 2 * half).astype(jnp.bfloat16)


def sort_words(words, sorted_words):
    rows = lax.broadcasted_iota(jnp.int32, (LANES, LANES), 0)
    lanes = lax.broadcasted_iota(jnp.int32, (LANES, LANES), 1)
    wanted = (rows // GROUP) == lanes % 4
    pick_row = lax.broadcasted_iota(jnp.int32, (GROUP, 2 * LANES), 0)
    pick_lane = lax.broadcasted_iota(jnp.int32, (GROUP, 2 * LANES), 1) % LANES
    pick = jnp.where(pick_row == pick_lane // 4, 1.0, 0.0).astype(jnp.bfloat16)
    for group in range(words.shape[0] // BLOCK):
        for h in range(2):
            part = words[pl.ds(group * BLOCK + h, GROUP, stride=2), :]
            low = (part & 255).astype(jnp.float32)
            high = (part - (part & 255)).astype(jnp.float32)
            both = jnp.concatenate(
                [
                    jnp.where(wanted, jnp.concatenate([half] * 4, axis=0), 0.0)
                    for half in (low, high)
                ],
                axis=1,
            ).astype(jnp.bfloat16)
            start = group * BLOCK + h * GROUP
            sorted_words[start : start + GROUP, :] = times_transposed(pick, both).astype(jnp.int32)


def greet(peer_count, mine_wide, mine, core, across):
    barrier = pltpu.get_barrier_semaphore()
    for step in range(1, peer_count):
        peer = lax.rem(mine_wide + step, peer_count)
        pl.semaphore_signal(barrier, inc=1, device_id=(peer, mine), device_id_type=MESH)
    for other in (core, across):
        pl.semaphore_signal(barrier, inc=1, device_id=(mine_wide, other), device_id_type=MESH)
    return barrier


def push(src, dst, send, recv, wide_to, rep_to):
    copy = pltpu.make_async_remote_copy(
        src_ref=src,
        dst_ref=dst,
        send_sem=send,
        recv_sem=recv,
        device_id=(wide_to, rep_to),
        device_id_type=MESH,
    )
    copy.start()
    return copy


def spread_inputs(
    peer_count,
    slots,
    words,
    tile_dst,
    tile_src,
    send_rows,
    feats,
    all_bits,
    all_meta,
    all_halo,
    bits,
    meta,
    outgoing,
    local_sem,
    send_sem,
    recv_sem,
    halo_send,
    halo_recv,
):
    mine_wide = lax.axis_index("wide")
    mine, core, across, diagonal = partners(4)
    barrier = greet(peer_count, mine_wide, mine, core, across)
    meta[...] = jnp.zeros_like(meta)
    meta[0:1, :] = tile_dst[...]
    meta[1:2, :] = tile_src[...]
    meta[8:, :slots] = send_rows[...]
    sort_words(words, bits)
    pl.semaphore_wait(barrier, peer_count + 1)

    pairs = ((bits, all_bits), (meta, all_meta))
    to_across = [
        push(src, dst.at[mine], send_sem.at[n], recv_sem.at[n], mine_wide, across)
        for n, (src, dst) in enumerate(pairs)
    ]
    to_core = [
        push(src, dst.at[mine], send_sem.at[3 + n], recv_sem.at[3 + n], mine_wide, core)
        for n, (src, dst) in enumerate(pairs)
    ]
    own = [
        pltpu.make_async_copy(src, dst.at[mine], local_sem.at[n])
        for n, (src, dst) in enumerate(pairs)
    ]
    for copy in own:
        copy.start()
    node_rows = feats.shape[0]
    for first in range(0, peer_count, 8):
        picks = as_column(send_rows[first : first + 8, :])
        chosen = picks == lax.broadcasted_iota(jnp.int32, (8 * slots, node_rows), 1)
        rows = jnp.dot(
            jnp.where(chosen, 1.0, 0.0).astype(jnp.bfloat16),
            feats[...],
            preferred_element_type=jnp.float32,
        )
        for n in range(8):
            outgoing[first + n] = folded(rows[n * slots : (n + 1) * slots])
    exchange = []
    for step in range(1, peer_count):
        peer = lax.rem(mine_wide + step, peer_count)
        exchange.append(
            push(
                outgoing.at[peer],
                all_halo.at[mine, mine_wide],
                halo_send.at[step],
                halo_recv.at[step],
                peer,
                mine,
            )
        )
    kept = pltpu.make_async_copy(
        outgoing.at[mine_wide], all_halo.at[mine, mine_wide], local_sem.at[2]
    )
    kept.start()
    kept.wait()
    for copy in exchange:
        copy.wait_recv()
    block = all_halo.at[mine]
    to_across.append(push(block, block, send_sem.at[2], recv_sem.at[2], mine_wide, across))
    to_core.append(push(block, block, send_sem.at[5], recv_sem.at[5], mine_wide, core))
    onward = []
    for n, dst in enumerate((all_bits, all_meta, all_halo)):
        to_across[n].wait_recv()
        block = dst.at[across]
        onward.append(push(block, block, send_sem.at[6 + n], recv_sem.at[6 + n], mine_wide, core))
    for copy in to_core + onward:
        copy.wait_recv()
    for copy in to_across + to_core + onward + exchange:
        copy.wait_send()
    for copy in own:
        copy.wait()


def build_adjacency(
    dst_count, halo_blocks, meta, bits, adjacency, low_sum, high_sum, lhs, raised_even, raised_odd
):
    replicas = bits.shape[0]
    per_sum = replicas // 2
    own_pairs = dst_count // 2
    halo_pairs = per_sum * halo_blocks // 2
    pair_count = own_pairs + halo_pairs
    groups = bits.shape[1] // BLOCK
    sums = (low_sum, high_sum)

    for target in sums:
        target[...] = jnp.zeros_like(target)
    for r in range(replicas):
        words = bits[r]
        rows = pl.ds(r * words.shape[0], words.shape[0])
        lhs[rows, :LANES] = (words & 255).astype(jnp.float32).astype(jnp.bfloat16)
        lhs[rows, LANES:] = (words >> 8).astype(jnp.float32).astype(jnp.bfloat16)

    row = lax.broadcasted_iota(jnp.int32, (2 * LANES, 2 * LANES), 0)
    col = lax.broadcasted_iota(jnp.int32, (2 * LANES, 2 * LANES), 1)
    bit = col & (BLOCK - 1)
    match = (((row >> 5) & 3) == (bit >> 4)) & ((row >> 7) == ((bit >> 3) & 1))
    factor = (1 << (7 - (bit & 7))).astype(jnp.float32) * (1.0 / 128.0)
    pattern = jnp.where(match, factor, 0.0)
    behind = (row & (GROUP - 1)) - (col >> 7)
    lane_half = lax.broadcasted_iota(jnp.int32, (1, LANES), 1) >> 6

    def expand(n):
        chosen = jnp.where(behind == 2 * n, pattern, 0.0).astype(jnp.bfloat16)
        return jnp.dot(lhs[...], chosen, preferred_element_type=jnp.float32)

    def add_tiles(raised, n):
        for g in range(groups):
            for t in range(2):
                for turn in range(replicas):
                    r = (turn % 2) * per_sum + turn // 2
                    place = g * GROUP + 2 * n + t
                    dst = meta[r, 0, place]
                    src = meta[r, 1, place]
                    column = jnp.where(src < dst_count, src, src + (r % per_sum) * halo_blocks)
                    where = dst * pair_count + (column >> 1)
                    keep = jnp.where(lane_half == (column & 1), 1, 0)
                    first = (r * groups + g) * BLOCK
                    part = raised[first : first + BLOCK, t * LANES : (t + 1) * LANES]
                    sums[r // per_sum][where] += (
                        (part.astype(jnp.int32) & keep).astype(jnp.float32).astype(jnp.bfloat16)
                    )

    raised_even[...] = expand(0)

    def four_tiles(m, carry):
        raised_odd[...] = expand(2 * m + 1)
        add_tiles(raised_even, 2 * m)
        raised_even[...] = expand(2 * m + 2)
        add_tiles(raised_odd, 2 * m + 1)
        return carry

    lax.fori_loop(0, GROUP // 4, four_tiles, 0)

    def place_row(b, carry):
        rows = pl.ds(pl.multiple_of(b * BLOCK, BLOCK), BLOCK)
        for p in range(own_pairs):
            both = low_sum[b * pair_count + p].astype(jnp.float32) + high_sum[
                b * pair_count + p
            ].astype(jnp.float32)
            adjacency[rows, p * LANES : (p + 1) * LANES] = both.astype(jnp.bfloat16)
        for n, target in enumerate(sums):
            for p in range(halo_pairs):
                start = (own_pairs + n * halo_pairs + p) * LANES
                adjacency[rows, start : start + LANES] = target[b * pair_count + own_pairs + p]
        return carry

    lax.fori_loop(0, dst_count, place_row, 0)


def layer(
    peer_count,
    slots,
    reduce_here,
    adjacency_from,
    halo,
    meta,
    grad_own,
    grad_core,
    grad_across,
    grad_diagonal,
    feats,
    w_self,
    w_neigh,
    norm,
    out_feats,
    grad_feats,
    weights,
    weight_grad,
    adjacency,
    table,
    scale,
    agg,
    grad_pre,
    grad_agg,
    halo_grad,
    halo_out,
    came_halo,
    came_weight,
    summed,
    local_sem,
    halo_send,
    halo_recv,
    part_send,
    part_recv,
    full_send,
    full_recv,
    rep_send,
    rep_recv,
    back_send,
    back_recv,
    fetch_sem,
):
    mine_wide = lax.axis_index("wide")
    mine, core, across, diagonal = partners(4)
    barrier = greet(peer_count, mine_wide, mine, core, across)
    replicas = meta.shape[0]
    node_rows, width = feats.shape
    halo_rows = peer_count * slots
    quarter = node_rows // replicas
    share = width // replicas
    rows = 2 * share // peer_count
    per_half = peer_count // 2

    def rows_of(q):
        return pl.ds(pl.multiple_of(q * quarter, quarter), quarter)

    fetches = [
        pltpu.make_async_copy(
            adjacency_from.at[rows_of(q)], adjacency.at[rows_of(q)], fetch_sem.at[n]
        )
        for n, q in enumerate((mine, core, across, diagonal))
    ]
    for copy in fetches:
        copy.start()
    table[:node_rows, :] = feats[...]
    for r in range(replicas):
        for first in range(0, peer_count, 8):
            start = node_rows + r * halo_rows + first * slots
            table[start : start + 8 * slots, :] = unfolded(halo[r, first : first + 8])
    eye = lax.broadcasted_iota(jnp.int32, (LANES, LANES), 0) == lax.broadcasted_iota(
        jnp.int32, (LANES, LANES), 1
    )
    for n in range(node_rows // LANES):
        counts = norm[n : n + 1, :].astype(jnp.float32)
        column = jnp.sum(jnp.where(eye, counts, 0.0), axis=1, keepdims=True)
        scale[n * LANES : (n + 1) * LANES, :] = lax.rsqrt(column)

    parts = ((mine, grad_own), (core, grad_core), (across, grad_across), (diagonal, grad_diagonal))
    for (q, grad_out), fetch in zip(parts, fetches):
        here = rows_of(q)
        fetch.wait()
        sums = jnp.dot(adjacency[here, :], table[...], preferred_element_type=jnp.float32)
        part_scale = scale[here, :]
        part_agg = (sums * part_scale).astype(jnp.bfloat16)
        agg[here, :] = part_agg
        pre = jnp.dot(feats[here, :], w_self[...], preferred_element_type=jnp.float32) + jnp.dot(
            part_agg, w_neigh[...], preferred_element_type=jnp.float32
        )
        sig = jax.nn.sigmoid(pre)
        if grad_out is grad_own:
            out_feats[...] = (pre * sig).astype(jnp.bfloat16)
        back = (grad_out[...].astype(jnp.float32) * sig * (1.0 + pre * (1.0 - sig))).astype(
            jnp.bfloat16
        )
        grad_pre[here, :] = back

    columns = pl.ds(pl.multiple_of(mine * share, share), share)
    weight_grad[:share, :] = transposed_times(feats[:, columns], grad_pre[...]).astype(
        jnp.bfloat16
    )
    weight_grad[share:, :] = transposed_times(agg[:, columns], grad_pre[...]).astype(jnp.bfloat16)
    pl.semaphore_wait(barrier, peer_count + 1)

    def place(owner_wide, owner_rep):
        start = owner_rep * share + lax.rem(owner_wide, per_half) * rows
        return weights.at[owner_wide // per_half, pl.ds(pl.multiple_of(start, rows), rows)]

    part_copies, halo_copies, full_copies = [], [], []
    if reduce_here:
        for step in range(1, peer_count):
            peer = lax.rem(mine_wide + step, peer_count)
            piece = weight_grad.at[pl.ds(pl.multiple_of(peer * rows, rows), rows)]
            part_copies.append(
                push(
                    piece, came_weight.at[step], part_send.at[step], part_recv.at[step], peer, mine
                )
            )

    grad_agg[...] = (times_transposed(grad_pre[...], w_neigh[...]) * scale[...]).astype(
        jnp.bfloat16
    )
    block = min(replicas * halo_rows, 512)
    for first in range(0, replicas * halo_rows, block):
        start = node_rows + first
        halo_grad[first : first + block, :] = transposed_times(
            adjacency[:, start : start + block], grad_agg[...]
        )
    for n in range(peer_count):
        start = pl.multiple_of(mine * halo_rows, 8) + n * slots
        halo_out[n] = folded(halo_grad[pl.ds(pl.multiple_of(start, 8), slots), :])
    for step in range(1, peer_count):
        peer = lax.rem(mine_wide + step, peer_count)
        halo_copies.append(
            push(
                halo_out.at[peer],
                came_halo.at[mine, mine_wide],
                halo_send.at[step],
                halo_recv.at[step],
                peer,
                mine,
            )
        )
    kept = pltpu.make_async_copy(
        halo_out.at[mine_wide], came_halo.at[mine, mine_wide], local_sem.at[0]
    )
    kept.start()
    own_rows = rows_of(mine)
    total_grad = transposed_times(adjacency[:, own_rows], grad_agg[...]) + times_transposed(
        grad_pre[own_rows, :], w_self[...]
    )

    if reduce_here:
        total = weight_grad[pl.ds(pl.multiple_of(mine_wide * rows, rows), rows), :].astype(
            jnp.float32
        )
        for step in range(1, peer_count):
            part_copies[step - 1].wait_recv()
            total = total + came_weight[step].astype(jnp.float32)
        summed[...] = total.astype(jnp.bfloat16)
        spot = place(mine_wide, mine)
        for step in range(1, peer_count):
            peer = lax.rem(mine_wide + step, peer_count)
            full_copies.append(
                push(summed, spot, full_send.at[step], full_recv.at[step], peer, mine)
            )
        across_copies = [
            push(summed, spot, rep_send.at[0, 0], rep_recv.at[0, 0], mine_wide, across)
        ]
        core_copies = [push(summed, spot, rep_send.at[1, 0], rep_recv.at[1, 0], mine_wide, core)]
        own_slice = pltpu.make_async_copy(summed, spot, local_sem.at[1])
        own_slice.start()

    kept.wait()
    for copy in halo_copies:
        copy.wait_recv()
    block = came_halo.at[mine]
    back_across = push(block, block, back_send.at[0], back_recv.at[0], mine_wide, across)
    back_core = push(block, block, back_send.at[1], back_recv.at[1], mine_wide, core)

    if reduce_here:
        for step in range(1, peer_count):
            full_copies[step - 1].wait_recv()
            owner = lax.rem(mine_wide + peer_count - step, peer_count)
            spot = place(owner, mine)
            across_copies.append(
                push(spot, spot, rep_send.at[0, step], rep_recv.at[0, step], mine_wide, across)
            )
            core_copies.append(
                push(spot, spot, rep_send.at[1, step], rep_recv.at[1, step], mine_wide, core)
            )

    back_across.wait_recv()
    block = came_halo.at[across]
    back_onward = push(block, block, back_send.at[2], back_recv.at[2], mine_wide, core)
    back_core.wait_recv()
    back_onward.wait_recv()
    for r in range(replicas):
        for first in range(0, peer_count, 8):
            picks = as_column(meta[r, 8 + first : 16 + first, :slots]) - mine * quarter
            chosen = picks == lax.broadcasted_iota(jnp.int32, (8 * slots, quarter), 1)
            total_grad = total_grad + transposed_times(
                jnp.where(chosen, 1.0, 0.0).astype(jnp.bfloat16),
                unfolded(came_halo[r, first : first + 8]),
            )
    grad_feats[...] = total_grad.astype(jnp.bfloat16)

    if reduce_here:
        onward = []
        for step in range(peer_count):
            across_copies[step].wait_recv()
            owner = lax.rem(mine_wide + peer_count - step, peer_count)
            spot = place(owner, across)
            onward.append(
                push(spot, spot, rep_send.at[2, step], rep_recv.at[2, step], mine_wide, core)
            )
        for copy in core_copies + onward:
            copy.wait_recv()
        for copy in part_copies + full_copies + across_copies + core_copies + onward:
            copy.wait_send()
        own_slice.wait()
    for copy in halo_copies + [back_across, back_core, back_onward]:
        copy.wait_send()


def deliver(out_feats, grad_feats, weights, out_to, grad_to, self_to, neigh_to, sems):
    pairs = (
        (out_feats, out_to),
        (grad_feats, grad_to),
        (weights.at[0], self_to),
        (weights.at[1], neigh_to),
    )
    copies = [pltpu.make_async_copy(src, dst, sems.at[n]) for n, (src, dst) in enumerate(pairs)]
    for copy in copies:
        copy.start()
    for copy in copies:
        copy.wait()


def on_device(
    node_feats, w_self, w_neigh, send_rows, tile_dst, tile_src, tile_bits, norm_count, grad_out
):
    node_rows, width = node_feats.shape
    peer_count = lax.axis_size("wide")
    replicas = lax.axis_size("rep")
    slots = send_rows.shape[2]
    tile_total = tile_dst.shape[2]
    quarter = node_rows // replicas
    halo_rows = peer_count * slots
    halo_blocks = halo_rows // BLOCK
    words = tile_bits.reshape(-1, LANES)
    any_spec = pl.BlockSpec(memory_space=pl.ANY)
    vmem_spec = pl.BlockSpec(memory_space=pltpu.VMEM)
    smem_spec = pl.BlockSpec(memory_space=pltpu.SMEM)

    def shaped(dims, held):
        return jax.ShapeDtypeStruct(dims, held)

    def dma(*dims):
        return pltpu.SemaphoreType.DMA(dims)

    by_core = [(n, n + 1 - 2 * (n % 2)) for n in range(replicas)]
    by_chip = [(n, (n + 2) % replicas) for n in range(replicas)]
    grad_across = lax.ppermute(grad_out, "rep", by_chip)
    grad_core = lax.ppermute(grad_out, "rep", by_core)
    grad_diagonal = lax.ppermute(grad_across, "rep", by_core)

    halo_shape = (replicas, peer_count, 2 * slots, width // 2)
    meta_shape = (8 + peer_count, tile_total)
    with jax.named_scope("spread_inputs"):
        all_bits, all_meta, all_halo = pl.pallas_call(
            functools.partial(spread_inputs, peer_count, slots),
            out_shape=(
                shaped((replicas,) + words.shape, jnp.int32),
                shaped((replicas,) + meta_shape, jnp.int32),
                shaped(halo_shape, jnp.bfloat16),
            ),
            in_specs=[vmem_spec] * 5,
            out_specs=(vmem_spec,) * 3,
            scratch_shapes=[
                pltpu.VMEM(words.shape, jnp.int32),
                pltpu.VMEM(meta_shape, jnp.int32),
                pltpu.VMEM(halo_shape[1:], jnp.bfloat16),
                dma(3),
                dma(9),
                dma(9),
                dma(peer_count),
                dma(peer_count),
            ],
            compiler_params=pltpu.CompilerParams(
                collective_id=0, has_side_effects=True, vmem_limit_bytes=VMEM_BYTES
            ),
        )(words, tile_dst[0], tile_src[0], send_rows[0], node_feats)

    columns = node_rows + replicas * halo_rows
    dst_count = node_rows // BLOCK
    sum_shape = (dst_count * (dst_count + replicas // 2 * halo_blocks) // 2, BLOCK, LANES)
    with jax.named_scope("build_adjacency"):
        adjacency = pl.pallas_call(
            functools.partial(build_adjacency, dst_count, halo_blocks),
            out_shape=shaped((node_rows, columns), jnp.bfloat16),
            in_specs=[smem_spec, vmem_spec],
            out_specs=vmem_spec,
            scratch_shapes=[
                pltpu.VMEM(sum_shape, jnp.bfloat16),
                pltpu.VMEM(sum_shape, jnp.bfloat16),
                pltpu.VMEM((replicas * words.shape[0], 2 * LANES), jnp.bfloat16),
                pltpu.VMEM((replicas * words.shape[0], 2 * LANES), jnp.float32),
                pltpu.VMEM((replicas * words.shape[0], 2 * LANES), jnp.float32),
            ],
            compiler_params=pltpu.CompilerParams(vmem_limit_bytes=VMEM_BYTES),
            cost_estimate=pl.CostEstimate(
                flops=8 * 10**9, bytes_accessed=4 * 10**6, transcendentals=0
            ),
        )(all_meta, all_bits)

    rows = 2 * width // replicas // peer_count
    reduce_here = rows % 16 == 0
    piece = (rows if reduce_here else 16, width)
    with jax.named_scope("layer"):
        out_feats, grad_feats, weights, weight_grad = pl.pallas_call(
            functools.partial(layer, peer_count, slots, reduce_here),
            out_shape=(
                shaped((quarter, width), jnp.bfloat16),
                shaped((quarter, width), jnp.bfloat16),
                shaped((2, width, width), jnp.bfloat16),
                shaped((2 * width // replicas, width), jnp.bfloat16),
            ),
            in_specs=[any_spec] + [vmem_spec] * 10,
            out_specs=(vmem_spec,) * 4,
            scratch_shapes=[
                pltpu.VMEM((node_rows, columns), jnp.bfloat16),
                pltpu.VMEM((columns, width), jnp.bfloat16),
                pltpu.VMEM((node_rows, 1), jnp.float32),
                pltpu.VMEM((node_rows, width), jnp.bfloat16),
                pltpu.VMEM((node_rows, width), jnp.bfloat16),
                pltpu.VMEM((node_rows, width), jnp.bfloat16),
                pltpu.VMEM((replicas * halo_rows, width), jnp.float32),
                pltpu.VMEM(halo_shape[1:], jnp.bfloat16),
                pltpu.VMEM(halo_shape, jnp.bfloat16),
                pltpu.VMEM((peer_count,) + piece, jnp.bfloat16),
                pltpu.VMEM(piece, jnp.bfloat16),
                dma(2),
            ]
            + [dma(peer_count)] * 6
            + [dma(3, peer_count)] * 2
            + [dma(3)] * 2
            + [dma(replicas)],
            compiler_params=pltpu.CompilerParams(
                collective_id=1, has_side_effects=True, vmem_limit_bytes=VMEM_BYTES
            ),
        )(
            adjacency,
            all_halo,
            all_meta,
            grad_out,
            grad_core,
            grad_across,
            grad_diagonal,
            node_feats,
            w_self,
            w_neigh,
            norm_count.reshape(-1, LANES),
        )
    if reduce_here:
        with jax.named_scope("deliver"):
            return pl.pallas_call(
                deliver,
                out_shape=(
                    shaped((quarter, width), jnp.bfloat16),
                    shaped((quarter, width), jnp.bfloat16),
                    shaped((width, width), jnp.bfloat16),
                    shaped((width, width), jnp.bfloat16),
                ),
                in_specs=[vmem_spec] * 3,
                out_specs=(any_spec,) * 4,
                scratch_shapes=[dma(4)],
            )(out_feats, grad_feats, weights)
    total = lax.psum(weight_grad.astype(jnp.float32), "wide").astype(jnp.bfloat16)
    whole = lax.all_gather(total, "rep", axis=0, tiled=False)
    share = width // replicas
    return (
        out_feats,
        grad_feats,
        whole[:, :share].reshape(width, width),
        whole[:, share:].reshape(width, width),
    )


def solution(mesh):
    in_specs = (
        P("wide", None),
        P(),
        P(),
        P("wide", None, "rep"),
        P("wide", "rep", None),
        P("wide", "rep", None),
        P("wide", "rep", None),
        P("wide"),
        P(("wide", "rep"), None),
    )
    out_specs = (P(("wide", "rep"), None), P(("wide", "rep"), None), P(), P())
    return jax.shard_map(
        on_device, mesh=mesh, in_specs=in_specs, out_specs=out_specs, check_vma=False
    )
```

```python
import functools

import jax
import jax.numpy as jnp
from jax import lax
from jax.experimental import pallas as pl
from jax.experimental.pallas import tpu as pltpu
from jax.sharding import PartitionSpec as P

BLOCK = 64
GROUP = 32
LANES = 128
MESH = pl.DeviceIdType.MESH
VMEM_BYTES = 56 * 1024 * 1024


def partners(replicas):
    mine = lax.axis_index("rep")
    core = mine + 1 - 2 * lax.rem(mine, 2)
    across = lax.rem(mine + 2, replicas)
    diagonal = lax.rem(core + 2, replicas)
    return mine, core, across, diagonal


def times_transposed(left, right):
    return lax.dot_general(
        left, right, (((1,), (1,)), ((), ())), preferred_element_type=jnp.float32
    )


def transposed_times(left, right):
    return lax.dot_general(
        left, right, (((0,), (0,)), ((), ())), preferred_element_type=jnp.float32
    )


def as_column(picks):
    count, slots = picks.shape
    same = lax.broadcasted_iota(jnp.int32, (count, slots, slots), 1) == lax.broadcasted_iota(
        jnp.int32, (count, slots, slots), 2
    )
    wide = jnp.broadcast_to(picks.astype(jnp.float32)[:, None, :], (count, slots, slots))
    column = jnp.sum(jnp.where(same, wide, 0.0), axis=2, keepdims=True)
    return column.reshape(count * slots, 1).astype(jnp.int32)


def folded(part):
    half = part.shape[1] // 2
    return jnp.concatenate([part[:, :half], part[:, half:]], axis=0).astype(jnp.bfloat16)


def unfolded(parts):
    count, rows, half = parts.shape
    wide = parts.astype(jnp.float32)
    joined = jnp.concatenate([wide[:, : rows // 2, :], wide[:, rows // 2 :, :]], axis=2)
    return joined.reshape(count * rows // 2, 2 * half).astype(jnp.bfloat16)


def sort_words(words, sorted_words):
    rows = lax.broadcasted_iota(jnp.int32, (LANES, LANES), 0)
    lanes = lax.broadcasted_iota(jnp.int32, (LANES, LANES), 1)
    wanted = (rows // GROUP) == lanes % 4
    pick_row = lax.broadcasted_iota(jnp.int32, (GROUP, 2 * LANES), 0)
    pick_lane = lax.broadcasted_iota(jnp.int32, (GROUP, 2 * LANES), 1) % LANES
    pick = jnp.where(pick_row == pick_lane // 4, 1.0, 0.0).astype(jnp.bfloat16)
    for group in range(words.shape[0] // BLOCK):
        for h in range(2):
            part = words[pl.ds(group * BLOCK + h, GROUP, stride=2), :]
            low = (part & 255).astype(jnp.float32)
            high = (part - (part & 255)).astype(jnp.float32)
            both = jnp.concatenate(
                [
                    jnp.where(wanted, jnp.concatenate([half] * 4, axis=0), 0.0)
                    for half in (low, high)
                ],
                axis=1,
            ).astype(jnp.bfloat16)
            start = group * BLOCK + h * GROUP
            sorted_words[start : start + GROUP, :] = times_transposed(pick, both).astype(jnp.int32)


def greet(peer_count, mine_wide, mine, core, across):
    barrier = pltpu.get_barrier_semaphore()
    for step in range(1, peer_count):
        peer = lax.rem(mine_wide + step, peer_count)
        pl.semaphore_signal(barrier, inc=1, device_id=(peer, mine), device_id_type=MESH)
    for other in (core, across):
        pl.semaphore_signal(barrier, inc=1, device_id=(mine_wide, other), device_id_type=MESH)
    return barrier


def push(src, dst, send, recv, wide_to, rep_to):
    copy = pltpu.make_async_remote_copy(
        src_ref=src,
        dst_ref=dst,
        send_sem=send,
        recv_sem=recv,
        device_id=(wide_to, rep_to),
        device_id_type=MESH,
    )
    copy.start()
    return copy


def spread_inputs(
    peer_count,
    slots,
    words,
    tile_dst,
    tile_src,
    send_rows,
    feats,
    all_bits,
    all_meta,
    all_halo,
    bits,
    meta,
    outgoing,
    local_sem,
    send_sem,
    recv_sem,
    halo_send,
    halo_recv,
):
    mine_wide = lax.axis_index("wide")
    mine, core, across, diagonal = partners(4)
    barrier = greet(peer_count, mine_wide, mine, core, across)
    meta[...] = jnp.zeros_like(meta)
    meta[0:1, :] = tile_dst[...]
    meta[1:2, :] = tile_src[...]
    meta[8:, :slots] = send_rows[...]
    sort_words(words, bits)
    pl.semaphore_wait(barrier, peer_count + 1)

    pairs = ((bits, all_bits), (meta, all_meta))
    to_across = [
        push(src, dst.at[mine], send_sem.at[n], recv_sem.at[n], mine_wide, across)
        for n, (src, dst) in enumerate(pairs)
    ]
    to_core = [
        push(src, dst.at[mine], send_sem.at[3 + n], recv_sem.at[3 + n], mine_wide, core)
        for n, (src, dst) in enumerate(pairs)
    ]
    own = [
        pltpu.make_async_copy(src, dst.at[mine], local_sem.at[n])
        for n, (src, dst) in enumerate(pairs)
    ]
    for copy in own:
        copy.start()
    node_rows = feats.shape[0]
    for first in range(0, peer_count, 8):
        picks = as_column(send_rows[first : first + 8, :])
        chosen = picks == lax.broadcasted_iota(jnp.int32, (8 * slots, node_rows), 1)
        rows = jnp.dot(
            jnp.where(chosen, 1.0, 0.0).astype(jnp.bfloat16),
            feats[...],
            preferred_element_type=jnp.float32,
        )
        for n in range(8):
            outgoing[first + n] = folded(rows[n * slots : (n + 1) * slots])
    exchange = []
    for step in range(1, peer_count):
        peer = lax.rem(mine_wide + step, peer_count)
        exchange.append(
            push(
                outgoing.at[peer],
                all_halo.at[mine, mine_wide],
                halo_send.at[step],
                halo_recv.at[step],
                peer,
                mine,
            )
        )
    kept = pltpu.make_async_copy(
        outgoing.at[mine_wide], all_halo.at[mine, mine_wide], local_sem.at[2]
    )
    kept.start()
    kept.wait()
    for copy in exchange:
        copy.wait_recv()
    block = all_halo.at[mine]
    to_across.append(push(block, block, send_sem.at[2], recv_sem.at[2], mine_wide, across))
    to_core.append(push(block, block, send_sem.at[5], recv_sem.at[5], mine_wide, core))
    onward = []
    for n, dst in enumerate((all_bits, all_meta, all_halo)):
        to_across[n].wait_recv()
        block = dst.at[across]
        onward.append(push(block, block, send_sem.at[6 + n], recv_sem.at[6 + n], mine_wide, core))
    for copy in to_core + onward:
        copy.wait_recv()
    for copy in to_across + to_core + onward + exchange:
        copy.wait_send()
    for copy in own:
        copy.wait()


def build_adjacency(
    dst_count, halo_blocks, meta, bits, adjacency, low_sum, high_sum, lhs, raised_even, raised_odd
):
    replicas = bits.shape[0]
    per_sum = replicas // 2
    own_pairs = dst_count // 2
    halo_pairs = per_sum * halo_blocks // 2
    pair_count = own_pairs + halo_pairs
    groups = bits.shape[1] // BLOCK
    sums = (low_sum, high_sum)

    for target in sums:
        target[...] = jnp.zeros_like(target)
    for r in range(replicas):
        words = bits[r]
        rows = pl.ds(r * words.shape[0], words.shape[0])
        lhs[rows, :LANES] = (words & 255).astype(jnp.float32).astype(jnp.bfloat16)
        lhs[rows, LANES:] = (words >> 8).astype(jnp.float32).astype(jnp.bfloat16)

    row = lax.broadcasted_iota(jnp.int32, (2 * LANES, 2 * LANES), 0)
    col = lax.broadcasted_iota(jnp.int32, (2 * LANES, 2 * LANES), 1)
    bit = col & (BLOCK - 1)
    match = (((row >> 5) & 3) == (bit >> 4)) & ((row >> 7) == ((bit >> 3) & 1))
    factor = (1 << (7 - (bit & 7))).astype(jnp.float32) * (1.0 / 128.0)
    pattern = jnp.where(match, factor, 0.0)
    behind = (row & (GROUP - 1)) - (col >> 7)
    lane_half = lax.broadcasted_iota(jnp.int32, (1, LANES), 1) >> 6

    def expand(n):
        chosen = jnp.where(behind == 2 * n, pattern, 0.0).astype(jnp.bfloat16)
        return jnp.dot(lhs[...], chosen, preferred_element_type=jnp.float32)

    def add_tiles(raised, n):
        for g in range(groups):
            for t in range(2):
                for turn in range(replicas):
                    r = (turn % 2) * per_sum + turn // 2
                    place = g * GROUP + 2 * n + t
                    dst = meta[r, 0, place]
                    src = meta[r, 1, place]
                    column = jnp.where(src < dst_count, src, src + (r % per_sum) * halo_blocks)
                    where = dst * pair_count + (column >> 1)
                    keep = jnp.where(lane_half == (column & 1), 1, 0)
                    first = (r * groups + g) * BLOCK
                    part = raised[first : first + BLOCK, t * LANES : (t + 1) * LANES]
                    sums[r // per_sum][where] += (
                        (part.astype(jnp.int32) & keep).astype(jnp.float32).astype(jnp.bfloat16)
                    )

    raised_even[...] = expand(0)

    def four_tiles(m, carry):
        raised_odd[...] = expand(2 * m + 1)
        add_tiles(raised_even, 2 * m)
        raised_even[...] = expand(2 * m + 2)
        add_tiles(raised_odd, 2 * m + 1)
        return carry

    lax.fori_loop(0, GROUP // 4, four_tiles, 0)

    def place_row(b, carry):
        rows = pl.ds(pl.multiple_of(b * BLOCK, BLOCK), BLOCK)
        for p in range(own_pairs):
            both = low_sum[b * pair_count + p].astype(jnp.float32) + high_sum[
                b * pair_count + p
            ].astype(jnp.float32)
            adjacency[rows, p * LANES : (p + 1) * LANES] = both.astype(jnp.bfloat16)
        for n, target in enumerate(sums):
            for p in range(halo_pairs):
                start = (own_pairs + n * halo_pairs + p) * LANES
                adjacency[rows, start : start + LANES] = target[b * pair_count + own_pairs + p]
        return carry

    lax.fori_loop(0, dst_count, place_row, 0)


def layer(
    peer_count,
    slots,
    reduce_here,
    adjacency_from,
    halo,
    meta,
    grad_own,
    grad_core,
    grad_across,
    grad_diagonal,
    feats,
    w_self,
    w_neigh,
    norm,
    out_feats,
    grad_feats,
    weights,
    weight_grad,
    adjacency,
    table,
    scale,
    agg,
    grad_pre,
    grad_agg,
    halo_grad,
    halo_out,
    came_halo,
    came_weight,
    summed,
    local_sem,
    halo_send,
    halo_recv,
    part_send,
    part_recv,
    full_send,
    full_recv,
    rep_send,
    rep_recv,
    back_send,
    back_recv,
    fetch_sem,
):
    mine_wide = lax.axis_index("wide")
    mine, core, across, diagonal = partners(4)
    barrier = greet(peer_count, mine_wide, mine, core, across)
    replicas = meta.shape[0]
    node_rows, width = feats.shape
    halo_rows = peer_count * slots
    quarter = node_rows // replicas
    share = width // replicas
    rows = 2 * share // peer_count
    per_half = peer_count // 2

    def rows_of(q):
        return pl.ds(pl.multiple_of(q * quarter, quarter), quarter)

    fetches = [
        pltpu.make_async_copy(
            adjacency_from.at[rows_of(q)], adjacency.at[rows_of(q)], fetch_sem.at[n]
        )
        for n, q in enumerate((mine, core, across, diagonal))
    ]
    for copy in fetches:
        copy.start()
    table[:node_rows, :] = feats[...]
    for r in range(replicas):
        for first in range(0, peer_count, 8):
            start = node_rows + r * halo_rows + first * slots
            table[start : start + 8 * slots, :] = unfolded(halo[r, first : first + 8])
    eye = lax.broadcasted_iota(jnp.int32, (LANES, LANES), 0) == lax.broadcasted_iota(
        jnp.int32, (LANES, LANES), 1
    )
    for n in range(node_rows // LANES):
        counts = norm[n : n + 1, :].astype(jnp.float32)
        column = jnp.sum(jnp.where(eye, counts, 0.0), axis=1, keepdims=True)
        scale[n * LANES : (n + 1) * LANES, :] = lax.rsqrt(column)

    parts = ((mine, grad_own), (core, grad_core), (across, grad_across), (diagonal, grad_diagonal))
    for (q, grad_out), fetch in zip(parts, fetches):
        here = rows_of(q)
        fetch.wait()
        sums = jnp.dot(adjacency[here, :], table[...], preferred_element_type=jnp.float32)
        part_scale = scale[here, :]
        part_agg = (sums * part_scale).astype(jnp.bfloat16)
        agg[here, :] = part_agg
        pre = jnp.dot(feats[here, :], w_self[...], preferred_element_type=jnp.float32) + jnp.dot(
            part_agg, w_neigh[...], preferred_element_type=jnp.float32
        )
        sig = jax.nn.sigmoid(pre)
        if grad_out is grad_own:
            out_feats[...] = (pre * sig).astype(jnp.bfloat16)
        back = (grad_out[...].astype(jnp.float32) * sig * (1.0 + pre * (1.0 - sig))).astype(
            jnp.bfloat16
        )
        grad_pre[here, :] = back

    columns = pl.ds(pl.multiple_of(mine * share, share), share)
    weight_grad[:share, :] = transposed_times(feats[:, columns], grad_pre[...]).astype(
        jnp.bfloat16
    )
    weight_grad[share:, :] = transposed_times(agg[:, columns], grad_pre[...]).astype(jnp.bfloat16)
    pl.semaphore_wait(barrier, peer_count + 1)

    def place(owner_wide, owner_rep):
        start = owner_rep * share + lax.rem(owner_wide, per_half) * rows
        return weights.at[owner_wide // per_half, pl.ds(pl.multiple_of(start, rows), rows)]

    part_copies, halo_copies, full_copies = [], [], []
    if reduce_here:
        for step in range(1, peer_count):
            peer = lax.rem(mine_wide + step, peer_count)
            piece = weight_grad.at[pl.ds(pl.multiple_of(peer * rows, rows), rows)]
            part_copies.append(
                push(
                    piece, came_weight.at[step], part_send.at[step], part_recv.at[step], peer, mine
                )
            )

    grad_agg[...] = (times_transposed(grad_pre[...], w_neigh[...]) * scale[...]).astype(
        jnp.bfloat16
    )
    block = min(replicas * halo_rows, 512)
    for first in range(0, replicas * halo_rows, block):
        start = node_rows + first
        halo_grad[first : first + block, :] = transposed_times(
            adjacency[:, start : start + block], grad_agg[...]
        )
    for n in range(peer_count):
        start = pl.multiple_of(mine * halo_rows, 8) + n * slots
        halo_out[n] = folded(halo_grad[pl.ds(pl.multiple_of(start, 8), slots), :])
    for step in range(1, peer_count):
        peer = lax.rem(mine_wide + step, peer_count)
        halo_copies.append(
            push(
                halo_out.at[peer],
                came_halo.at[mine, mine_wide],
                halo_send.at[step],
                halo_recv.at[step],
                peer,
                mine,
            )
        )
    kept = pltpu.make_async_copy(
        halo_out.at[mine_wide], came_halo.at[mine, mine_wide], local_sem.at[0]
    )
    kept.start()
    if reduce_here:
        total = weight_grad[pl.ds(pl.multiple_of(mine_wide * rows, rows), rows), :].astype(
            jnp.float32
        )
        for step in range(1, peer_count):
            part_copies[step - 1].wait_recv()
            total = total + came_weight[step].astype(jnp.float32)
        summed[...] = total.astype(jnp.bfloat16)
        spot = place(mine_wide, mine)
        for step in range(1, peer_count):
            peer = lax.rem(mine_wide + step, peer_count)
            full_copies.append(
                push(summed, spot, full_send.at[step], full_recv.at[step], peer, mine)
            )
        across_copies = [
            push(summed, spot, rep_send.at[0, 0], rep_recv.at[0, 0], mine_wide, across)
        ]
        core_copies = [push(summed, spot, rep_send.at[1, 0], rep_recv.at[1, 0], mine_wide, core)]
        own_slice = pltpu.make_async_copy(summed, spot, local_sem.at[1])
        own_slice.start()

    kept.wait()
    for copy in halo_copies:
        copy.wait_recv()
    block = came_halo.at[mine]
    back_across = push(block, block, back_send.at[0], back_recv.at[0], mine_wide, across)
    back_core = push(block, block, back_send.at[1], back_recv.at[1], mine_wide, core)

    if reduce_here:
        for step in range(1, peer_count):
            full_copies[step - 1].wait_recv()
            owner = lax.rem(mine_wide + peer_count - step, peer_count)
            spot = place(owner, mine)
            across_copies.append(
                push(spot, spot, rep_send.at[0, step], rep_recv.at[0, step], mine_wide, across)
            )
            core_copies.append(
                push(spot, spot, rep_send.at[1, step], rep_recv.at[1, step], mine_wide, core)
            )

    own_rows = rows_of(mine)
    total_grad = transposed_times(adjacency[:, own_rows], grad_agg[...]) + times_transposed(
        grad_pre[own_rows, :], w_self[...]
    )

    back_across.wait_recv()
    block = came_halo.at[across]
    back_onward = push(block, block, back_send.at[2], back_recv.at[2], mine_wide, core)
    back_core.wait_recv()
    back_onward.wait_recv()
    for r in range(replicas):
        for first in range(0, peer_count, 8):
            picks = as_column(meta[r, 8 + first : 16 + first, :slots]) - mine * quarter
            chosen = picks == lax.broadcasted_iota(jnp.int32, (8 * slots, quarter), 1)
            total_grad = total_grad + transposed_times(
                jnp.where(chosen, 1.0, 0.0).astype(jnp.bfloat16),
                unfolded(came_halo[r, first : first + 8]),
            )
    grad_feats[...] = total_grad.astype(jnp.bfloat16)

    if reduce_here:
        onward = []
        for step in range(peer_count):
            across_copies[step].wait_recv()
            owner = lax.rem(mine_wide + peer_count - step, peer_count)
            spot = place(owner, across)
            onward.append(
                push(spot, spot, rep_send.at[2, step], rep_recv.at[2, step], mine_wide, core)
            )
        for copy in core_copies + onward:
            copy.wait_recv()
        for copy in part_copies + full_copies + across_copies + core_copies + onward:
            copy.wait_send()
        own_slice.wait()
    for copy in halo_copies + [back_across, back_core, back_onward]:
        copy.wait_send()


def deliver(out_feats, grad_feats, weights, out_to, grad_to, self_to, neigh_to, sems):
    pairs = (
        (out_feats, out_to),
        (grad_feats, grad_to),
        (weights.at[0], self_to),
        (weights.at[1], neigh_to),
    )
    copies = [pltpu.make_async_copy(src, dst, sems.at[n]) for n, (src, dst) in enumerate(pairs)]
    for copy in copies:
        copy.start()
    for copy in copies:
        copy.wait()


def on_device(
    node_feats, w_self, w_neigh, send_rows, tile_dst, tile_src, tile_bits, norm_count, grad_out
):
    node_rows, width = node_feats.shape
    peer_count = lax.axis_size("wide")
    replicas = lax.axis_size("rep")
    slots = send_rows.shape[2]
    tile_total = tile_dst.shape[2]
    quarter = node_rows // replicas
    halo_rows = peer_count * slots
    halo_blocks = halo_rows // BLOCK
    words = tile_bits.reshape(-1, LANES)
    any_spec = pl.BlockSpec(memory_space=pl.ANY)
    vmem_spec = pl.BlockSpec(memory_space=pltpu.VMEM)
    smem_spec = pl.BlockSpec(memory_space=pltpu.SMEM)

    def shaped(dims, held):
        return jax.ShapeDtypeStruct(dims, held)

    def dma(*dims):
        return pltpu.SemaphoreType.DMA(dims)

    by_core = [(n, n + 1 - 2 * (n % 2)) for n in range(replicas)]
    by_chip = [(n, (n + 2) % replicas) for n in range(replicas)]
    grad_across = lax.ppermute(grad_out, "rep", by_chip)
    grad_core = lax.ppermute(grad_out, "rep", by_core)
    grad_diagonal = lax.ppermute(grad_across, "rep", by_core)

    halo_shape = (replicas, peer_count, 2 * slots, width // 2)
    meta_shape = (8 + peer_count, tile_total)
    with jax.named_scope("spread_inputs"):
        all_bits, all_meta, all_halo = pl.pallas_call(
            functools.partial(spread_inputs, peer_count, slots),
            out_shape=(
                shaped((replicas,) + words.shape, jnp.int32),
                shaped((replicas,) + meta_shape, jnp.int32),
                shaped(halo_shape, jnp.bfloat16),
            ),
            in_specs=[vmem_spec] * 5,
            out_specs=(vmem_spec,) * 3,
            scratch_shapes=[
                pltpu.VMEM(words.shape, jnp.int32),
                pltpu.VMEM(meta_shape, jnp.int32),
                pltpu.VMEM(halo_shape[1:], jnp.bfloat16),
                dma(3),
                dma(9),
                dma(9),
                dma(peer_count),
                dma(peer_count),
            ],
            compiler_params=pltpu.CompilerParams(
                collective_id=0, has_side_effects=True, vmem_limit_bytes=VMEM_BYTES
            ),
        )(words, tile_dst[0], tile_src[0], send_rows[0], node_feats)

    columns = node_rows + replicas * halo_rows
    dst_count = node_rows // BLOCK
    sum_shape = (dst_count * (dst_count + replicas // 2 * halo_blocks) // 2, BLOCK, LANES)
    with jax.named_scope("build_adjacency"):
        adjacency = pl.pallas_call(
            functools.partial(build_adjacency, dst_count, halo_blocks),
            out_shape=shaped((node_rows, columns), jnp.bfloat16),
            in_specs=[smem_spec, vmem_spec],
            out_specs=vmem_spec,
            scratch_shapes=[
                pltpu.VMEM(sum_shape, jnp.bfloat16),
                pltpu.VMEM(sum_shape, jnp.bfloat16),
                pltpu.VMEM((replicas * words.shape[0], 2 * LANES), jnp.bfloat16),
                pltpu.VMEM((replicas * words.shape[0], 2 * LANES), jnp.float32),
                pltpu.VMEM((replicas * words.shape[0], 2 * LANES), jnp.float32),
            ],
            compiler_params=pltpu.CompilerParams(vmem_limit_bytes=VMEM_BYTES),
            cost_estimate=pl.CostEstimate(
                flops=8 * 10**9, bytes_accessed=4 * 10**6, transcendentals=0
            ),
        )(all_meta, all_bits)

    rows = 2 * width // replicas // peer_count
    reduce_here = rows % 16 == 0
    piece = (rows if reduce_here else 16, width)
    with jax.named_scope("layer"):
        out_feats, grad_feats, weights, weight_grad = pl.pallas_call(
            functools.partial(layer, peer_count, slots, reduce_here),
            out_shape=(
                shaped((quarter, width), jnp.bfloat16),
                shaped((quarter, width), jnp.bfloat16),
                shaped((2, width, width), jnp.bfloat16),
                shaped((2 * width // replicas, width), jnp.bfloat16),
            ),
            in_specs=[any_spec] + [vmem_spec] * 10,
            out_specs=(vmem_spec,) * 4,
            scratch_shapes=[
                pltpu.VMEM((node_rows, columns), jnp.bfloat16),
                pltpu.VMEM((columns, width), jnp.bfloat16),
                pltpu.VMEM((node_rows, 1), jnp.float32),
                pltpu.VMEM((node_rows, width), jnp.bfloat16),
                pltpu.VMEM((node_rows, width), jnp.bfloat16),
                pltpu.VMEM((node_rows, width), jnp.bfloat16),
                pltpu.VMEM((replicas * halo_rows, width), jnp.float32),
                pltpu.VMEM(halo_shape[1:], jnp.bfloat16),
                pltpu.VMEM(halo_shape, jnp.bfloat16),
                pltpu.VMEM((peer_count,) + piece, jnp.bfloat16),
                pltpu.VMEM(piece, jnp.bfloat16),
                dma(2),
            ]
            + [dma(peer_count)] * 6
            + [dma(3, peer_count)] * 2
            + [dma(3)] * 2
            + [dma(replicas)],
            compiler_params=pltpu.CompilerParams(
                collective_id=1, has_side_effects=True, vmem_limit_bytes=VMEM_BYTES
            ),
        )(
            adjacency,
            all_halo,
            all_meta,
            grad_out,
            grad_core,
            grad_across,
            grad_diagonal,
            node_feats,
            w_self,
            w_neigh,
            norm_count.reshape(-1, LANES),
        )
    if reduce_here:
        with jax.named_scope("deliver"):
            return pl.pallas_call(
                deliver,
                out_shape=(
                    shaped((quarter, width), jnp.bfloat16),
                    shaped((quarter, width), jnp.bfloat16),
                    shaped((width, width), jnp.bfloat16),
                    shaped((width, width), jnp.bfloat16),
                ),
                in_specs=[vmem_spec] * 3,
                out_specs=(any_spec,) * 4,
                scratch_shapes=[dma(4)],
            )(out_feats, grad_feats, weights)
    total = lax.psum(weight_grad.astype(jnp.float32), "wide").astype(jnp.bfloat16)
    whole = lax.all_gather(total, "rep", axis=0, tiled=False)
    share = width // replicas
    return (
        out_feats,
        grad_feats,
        whole[:, :share].reshape(width, width),
        whole[:, share:].reshape(width, width),
    )


def solution(mesh):
    in_specs = (
        P("wide", None),
        P(),
        P(),
        P("wide", None, "rep"),
        P("wide", "rep", None),
        P("wide", "rep", None),
        P("wide", "rep", None),
        P("wide"),
        P(("wide", "rep"), None),
    )
    out_specs = (P(("wide", "rep"), None), P(("wide", "rep"), None), P(), P())
    return jax.shard_map(
        on_device, mesh=mesh, in_specs=in_specs, out_specs=out_specs, check_vma=False
    )
```
